128 devices in a mesh: rows: 16 (over z_hi, y, core), cols: 8 (over z_lo, x).
Axes of the slice: x: 4, y: 4, z: 4 (z_hi: 2, z_lo: 2; z = z_hi * 2 + z_lo), core: 2. Of those that a mesh axis runs over, the one named last changes fastest.
Arguments:
- field_real: float32 [6144, 6144], P('rows', 'cols'), may hold values from -6 to 6
- field_imag: float32 [6144, 6144], P('rows', 'cols'), may hold values from -6 to 6
- kerr_map: float32 [6144, 6144], P('rows', 'cols'), may hold values from 0.1 to 1
- pinhole: int32 [6144, 6144], P(None, ('rows', 'cols')), may hold values from 0 to 1, as said below
Outputs:
- out_real: float32 [6144, 6144], P('rows', 'cols')
- out_imag: float32 [6144, 6144], P('rows', 'cols')
- b_integral: float32 [6144, 6144], P('rows', 'cols')
The draws below stay inside these ranges and needn't reach their ends.
Inputs may be any that keep to these rules, and one draw needn't show every extreme that they name: pinhole is 1 at every far-field pixel whose frequency (indices above 3072 taken as negative, so the disc wraps to the corners) lies inside a disc about zero frequency of radius R, and 0 outside it, except within about two pixels of the disc's rim, where it may take either value; R lies between 1536 and 2048 and varies from draw to draw.
All inputs are finite; a program needn't handle non-finite values.
Results may differ from the reference program's by a relative error of at most 0.00014.
Values sent between devices are 32-bit elements; how exact they have to be, the bound alone decides.
No kernel may reach another device: no remote copies, remote signals or barrier semaphores. Data moves between devices by JAX's collectives and lax.ppermute only.
A program may use at most 192 MiB of HBM per device.

```python
import math
import jax
import jax.numpy as jnp
from jax import lax

N = 6144


def draw_pinhole(key, part):
    base = jax.random.fold_in(key, 17)
    radius_key = jax.random.fold_in(base, 1)
    flip_key = jax.random.fold_in(base, 2)
    radius = jax.random.randint(radius_key, (), N // 4, N // 3 + 1).astype(jnp.int32)
    index = jnp.arange(N, dtype=jnp.int32)
    freq = jnp.minimum(index, N - index)
    dist = freq[:, None] * freq[:, None] + freq[None, :] * freq[None, :]
    limit = radius * radius
    inside = (dist <= limit).astype(jnp.int32)
    near_rim = jnp.abs(dist - limit) <= 4 * radius
    flips = jax.random.randint(flip_key, (N, N), 0, 2).astype(jnp.int32)
    return jnp.where(near_rim, flips, inside).astype(jnp.int32)


def block_levels(own_key, dims, split, least, high):
    loudness = 1.0
    for axis_at, blocks in split:
        steps = jax.random.uniform(jax.random.fold_in(jax.random.fold_in(own_key, 6), axis_at), (blocks,), jnp.float32, least / len(split), high / len(split))
        loudness = loudness * jnp.repeat(jnp.exp(steps), dims[axis_at] // blocks).reshape((-1,) + (1,) * (len(dims) - 1 - axis_at))
    return loudness


def scatter_about(key, shape, width, bound, split=(), held_as=jnp.bfloat16):
    gain = block_levels(key, shape, split, -0.22, 0.18) if split else 1.0
    entries = jax.random.normal(key, shape, jnp.float32) * width * gain
    return jnp.minimum(jnp.maximum(entries, -bound), bound).astype(held_as)


def setup_inputs(seed: int = 0) -> dict:
    splits = jax.random.split(jax.random.key(seed), 5)
    field_real = scatter_about(splits[0], (N, N), 0.7071, 6.0, ((0, 16), (1, 8)), jnp.float32)
    field_imag = scatter_about(splits[1], (N, N), 0.7071, 6.0, ((0, 16), (1, 8)), jnp.float32)
    kerr_map = jnp.clip(jnp.exp(math.log(1.0) - 2.3025851 * jax.random.uniform(splits[2], (N, N), jnp.float32) ** block_levels(splits[2], (N, N), ((0, 16), (1, 8)), -0.2, 0.2)), 0.1, 1.0)
    pinhole = draw_pinhole(jax.random.fold_in(splits[4], 71), 0)
    return {"field_real": field_real, "field_imag": field_imag, "kerr_map": kerr_map, "pinhole": pinhole}


def kerr_phase(real_part, imag_part, kerr_map):
    power = real_part * real_part + imag_part * imag_part
    phase = kerr_map * power
    cosine = jnp.cos(phase)
    sine = jnp.sin(phase)
    return real_part * cosine - imag_part * sine, real_part * sine + imag_part * cosine, phase


def chirp_angle():
    index = jnp.arange(N, dtype=jnp.int32)
    squares = (index * index) % (2 * N)
    total = (squares[:, None] + squares[None, :]) % (2 * N)
    return -(math.pi / N) * total.astype(jnp.float32)


def propagate(real_part, imag_part, angle):
    field = lax.complex(real_part, imag_part)
    spectrum = jnp.fft.fft2(field, norm="ortho")
    spectrum = spectrum * lax.complex(jnp.cos(angle), jnp.sin(angle))
    back = jnp.fft.ifft2(spectrum, norm="ortho")
    return jnp.real(back), jnp.imag(back)


def reference(field_real, field_imag, kerr_map, pinhole):
    angle = chirp_angle()
    real_part, imag_part, phase_one = kerr_phase(field_real, field_imag, kerr_map)
    real_part, imag_part = propagate(real_part, imag_part, angle)
    real_part, imag_part, phase_two = kerr_phase(real_part, imag_part, kerr_map)
    real_part, imag_part = propagate(real_part, imag_part, angle)
    field = lax.complex(real_part, imag_part)
    spectrum = jnp.fft.fft2(field, norm="ortho") * pinhole.astype(jnp.float32)
    image = jnp.fft.ifft2(spectrum, norm="ortho")
    image = jnp.roll(jnp.flip(image, (0, 1)), 1, (0, 1))
    return jnp.real(image), jnp.imag(image), phase_one + phase_two
```

```python
import math

import jax
import jax.numpy as jnp
import ml_dtypes
import numpy as np
from jax import lax
from jax.experimental import pallas as pl
from jax.experimental.pallas import tpu as pltpu
from jax.sharding import PartitionSpec as P

N = 6144
DEV = 128
PITCH = 40
F32 = jnp.float32
BF16 = jnp.bfloat16
NT = (((1,), (1,)), ((), ()))
NN = (((1,), (0,)), ((), ()))
VMEM_LIMIT = 56 * 1024 * 1024


def root(period, product):
    return np.exp(-2j * np.pi * (np.asarray(product) % period) / period)


def real_form(matrix):
    return np.block([[matrix.real, -matrix.imag], [matrix.imag, matrix.real]])


def halves(matrix):
    high = matrix.astype(np.float32).astype(ml_dtypes.bfloat16)
    low = (matrix - high.astype(np.float64)).astype(ml_dtypes.bfloat16)
    return np.stack([high, low])


def planes(table):
    return np.stack([table.real, table.imag]).astype(np.float32)


def make_tables():
    t = {}
    r128 = np.arange(128)
    n1_of_src = 16 * (r128 % 8) + r128 // 8
    s128 = 1 / math.sqrt(128)
    s48 = 1 / math.sqrt(48)
    d_hi, jj, d_lo = np.meshgrid(np.arange(16), np.arange(3), np.arange(8), indexing="ij")
    k = (3 * (8 * d_hi + d_lo) + jj).reshape(-1)
    d384 = root(384, k[:, None] * np.arange(384)[None, :]) / math.sqrt(N)
    t["d384"] = halves(real_form(d384))
    q16 = np.arange(16)
    t["tw1"] = planes(root(N, q16[:, None] * np.arange(384)[None, :]).reshape(16, 1, 384))
    t["l_mixed"] = halves(real_form(root(128, r128[:, None] * n1_of_src[None, :]) * s128))
    t["l_plain"] = halves(real_form(root(128, r128[:, None] * r128[None, :]) * s128))
    lane_q, lane_8 = r128 // 8, r128 % 8
    row_8, row_q = r128 // 16, r128 % 16
    same = (row_q[:, None] == lane_q[None, :]).astype(np.float64)
    g6 = np.arange(6)[:, None, None]
    first = same * root(48, lane_8[None, None, :] * g6 + 6 * row_8[None, :, None] * lane_8[None, None, :]) * s48
    t["m_first"] = np.stack([halves(real_form(m)) for m in first], 1)
    second = same.T * root(48, g6 * lane_8[None, :, None] + 6 * row_8[None, None, :] * lane_8[None, :, None]) * s48
    t["m_second"] = np.stack([halves(real_form(m)) for m in second], 1)
    a = lane_8[None, :] + 8 * np.arange(6)[:, None]
    tw = root(N, r128[None, :, None] * a[:, None, :])
    t["tw_u_a"] = planes(tw)
    t["tw_a_u"] = planes(tw.transpose(0, 2, 1))
    keep = (lane_8[:, None] == lane_8[None, :]).astype(np.float64)
    v3 = np.arange(3)[:, None, None]
    into = keep * root(48, lane_q[None, :, None] * v3 + 3 * lane_q[None, :, None] * lane_q[None, None, :]) * s48
    t["r_in"] = np.stack([halves(real_form(m.T).T) for m in into], 1)
    back = keep * root(48, lane_q[None, None, :] * v3 + 3 * lane_q[None, :, None] * lane_q[None, None, :]) * s48
    t["r_out"] = np.stack([halves(real_form(m.T).T) for m in back], 1)
    rho = lane_q[None, :] + 16 * np.arange(3)[:, None]
    t["tw_u_rho"] = planes(root(N, r128[None, :, None] * rho[:, None, :]))
    kx = r128[None, :, None] + 128 * (np.arange(3)[:, None, None] + 3 * lane_q[None, None, :])
    t["h_x"] = planes(root(2 * N, kx * kx))
    y = r128[None, None, :] + 128 * (np.arange(6)[:, None, None] + 6 * row_8[None, :, None])
    t["chirp_y"] = (math.pi / N * ((y * y + N) % (2 * N) - N)).astype(np.float32)
    return t


TABLES = make_tables()


def chirp_angle(index):
    return math.pi / N * ((index * index + N) % (2 * N) - N).astype(F32)


def sin_cos(angle):
    turns = jnp.floor(angle * (2.0 / math.pi) + 0.5)
    r = angle - turns * 1.5703125
    r = r - turns * 4.837512969970703e-4
    r = r - turns * 7.549789948768648e-8
    quarter = turns.astype(jnp.int32)
    r2 = r * r
    sine = r + r * r2 * (-1.6666654611e-1 + r2 * (8.3321608736e-3 + r2 * -1.9515295891e-4))
    cosine = 1.0 - 0.5 * r2 + r2 * r2 * (4.166664568298827e-2 + r2 * (-1.388731625493765e-3 + r2 * 2.443315711809948e-5))
    odd = (quarter & 1) == 1
    s = jnp.where(odd, cosine, sine)
    c = jnp.where(odd, sine, cosine)
    s = jnp.where((quarter & 2) == 2, -s, s)
    c = jnp.where(((quarter + 1) & 2) == 2, -c, c)
    return s, c


def split(x):
    high = x.astype(BF16)
    return high, (x - high.astype(F32)).astype(BF16)


def mm(a, b, dims):
    return lax.dot_general(a, b, dims, preferred_element_type=F32)


def dot_left(table, data, dims):
    return mm(table[0], data[0], dims) + (mm(table[0], data[1], dims) + mm(table[1], data[0], dims))


def dot_right(data, table, dims):
    return mm(data[0], table[0], dims) + (mm(data[1], table[0], dims) + mm(data[0], table[1], dims))


def turn(z, w):
    return (z[0] * w[0] - z[1] * w[1], z[0] * w[1] + z[1] * w[0])


def add(a, b):
    return (a[0] + b[0], a[1] + b[1])


def sub(a, b):
    return (a[0] - b[0], a[1] - b[1])


def minus_i(a):
    return (a[1], -a[0])


def by_const(a, w):
    return (a[0] * w.real - a[1] * w.imag, a[0] * w.imag + a[1] * w.real)


def dft2(a, b):
    return add(a, b), sub(a, b)


def dft3(a, b, c):
    s = add(b, c)
    d = sub(b, c)
    h = math.sqrt(0.75)
    m = (a[0] - 0.5 * s[0], a[1] - 0.5 * s[1])
    e = (h * d[1], -h * d[0])
    return add(a, s), add(m, e), sub(m, e)


def dft4(a, b, c, d):
    p, q = dft2(a, c)
    r, s = dft2(b, d)
    s = minus_i(s)
    return add(p, r), add(q, s), sub(p, r), sub(q, s)


def dft6(z):
    even = dft3(z[0], z[2], z[4])
    odd = dft3(z[3], z[5], z[1])
    out = [None] * 6
    for k in range(6):
        f = add if k % 2 == 0 else sub
        out[k] = f(even[k % 3], odd[k % 3])
    return out


def dft16(z):
    cols = [dft4(z[i], z[i + 4], z[i + 8], z[i + 12]) for i in range(4)]
    out = [None] * 16
    for k1 in range(4):
        row = []
        for i in range(4):
            e = (i * k1) % 16
            row.append(cols[i][k1] if e == 0 else by_const(cols[i][k1], np.exp(-2j * np.pi * e / 16)))
        res = dft4(*row)
        for k2 in range(4):
            out[k1 + 4 * k2] = res[k2]
    return out


def enter_kernel(re_ref, im_ref, kerr_ref, ax_ref, ay_ref, out_ref, phase_ref):
    def body(jb, _):
        rows = pl.ds(pl.multiple_of(jb * 128, 128), 128)
        for lb in range(6):
            cols = slice(128 * lb, 128 * lb + 128)
            re, im = re_ref[rows, cols], im_ref[rows, cols]
            phase = kerr_ref[rows, cols] * (re * re + im * im)
            phase_ref[rows, cols] = phase
            s, c = sin_cos(phase + (ax_ref[rows, :] + ay_ref[:, cols]))
            both = turn((re, im), (c, s))
            for p in range(2):
                turned = both[p].T
                for i in range(8):
                    l = 128 * lb + 16 * i
                    out_ref[l // 48, pl.ds(48 * p + l % 48, 16), rows] = turned[16 * i:16 * i + 16]
        return 0

    lax.fori_loop(0, 3, body, 0)


def columns_kernel(in_ref, d_ref, tw_ref, out_ref, high_ref, low_ref):
    for lh in range(6):
        for t in range(3):
            lanes = slice(128 * t, 128 * t + 128)
            z = [(in_ref[r, 8 * lh:8 * lh + 8, lanes], in_ref[r, 48 + 8 * lh:56 + 8 * lh, lanes]) for r in range(16)]
            z = dft16(z)
            z = [z[0]] + [turn(z[q], (tw_ref[0, q, :, lanes], tw_ref[1, q, :, lanes])) for q in range(1, 16)]
            for q in range(0, 16, 2):
                rows = slice(128 * lh + 8 * q, 128 * lh + 8 * q + 16)
                for p in range(2):
                    h, l = split(jnp.concatenate([z[q][p], z[q + 1][p]], 0))
                    where = slice(384 * p + 128 * t, 384 * p + 128 * t + 128)
                    high_ref[rows, where] = h
                    low_ref[rows, where] = l
        rows = slice(128 * lh, 128 * lh + 128)
        res = dot_left((d_ref[0], d_ref[1]), (high_ref[rows, :], low_ref[rows, :]), NT)
        for p in range(2):
            for dh in range(16):
                for j in range(3):
                    at = 384 * p + 24 * dh + 8 * j
                    start = dh * 8 * PITCH + 12 * j + 6 * p + lh
                    out_ref[pl.ds(start, 8, stride=PITCH), :] = res[at:at + 8]


def gather_rows(in_ref, row):
    return in_ref[pl.ds(row, 128, stride=PITCH), :]


def over_senders(in_ref, base, tiles, table, out_ref):
    data = jnp.concatenate(
        [jnp.concatenate([gather_rows(in_ref, base + off), gather_rows(in_ref, base + off + 6)], 0) for off in tiles], 1
    )
    out_ref[...] = dot_left(table, split(data), NN)


def rows_first(in_ref, j, l_ref, tw_ref, y_ref, high_ref, low_ref):
    over_senders(in_ref, 12 * j, range(6), (l_ref[0], l_ref[1]), y_ref)
    for u in range(0, 128, 16):
        z = []
        for t in range(6):
            lanes = slice(128 * t, 128 * t + 128)
            w = (tw_ref[0, t, u:u + 16, :], tw_ref[1, t, u:u + 16, :])
            z.append(turn((y_ref[u:u + 16, lanes], y_ref[128 + u:144 + u, lanes]), w))
        z = dft6(z)
        for t in range(6):
            for p in range(2):
                h, l = split(z[t][p])
                high_ref[t, u:u + 16, 128 * p:128 * p + 128] = h
                low_ref[t, u:u + 16, 128 * p:128 * p + 128] = l


def rows_kernel(in_ref, kerr_ref, ax_ref, ay_ref, l_ref, m_ref, m2_ref, l2_ref, tw_ref, tw2_ref,
                out_ref, phase_ref, y_ref, w_ref, high_ref, low_ref):
    def body(j, _):
        rows_first(in_ref, j, l_ref, tw_ref, y_ref, high_ref, low_ref)
        rows = pl.ds(pl.multiple_of(16 * j, 16), 16)
        ax = ax_ref[pl.ds(pl.multiple_of(128 * j, 128), 128), :]
        for t in range(6):
            z = dot_left((m_ref[0, t], m_ref[1, t]), (high_ref[t], low_ref[t]), NT)
            re, im = z[:128], z[128:]
            lanes = slice(128 * t, 128 * t + 128)
            phase = kerr_ref[:, rows, lanes].reshape(128, 128) * (re * re + im * im)
            phase_ref[:, rows, lanes] = phase.reshape(8, 16, 128)
            s, c = sin_cos(phase + (ax + ay_ref[t]))
            both = jnp.concatenate(turn((im, -re), (c, s)), 0)
            w_ref[t] = dot_left((m2_ref[0, t], m2_ref[1, t]), split(both), NN)
        for r in range(0, 128, 16):
            z = dft6([(w_ref[t, r:r + 16, :], w_ref[t, 128 + r:144 + r, :]) for t in range(6)])
            for t in range(6):
                q = turn(z[t], (tw2_ref[0, t, r:r + 16, :], tw2_ref[1, t, r:r + 16, :]))
                for p in range(2):
                    h, l = split(q[p])
                    high_ref[t, r:r + 16, 128 * p:128 * p + 128] = h
                    low_ref[t, r:r + 16, 128 * p:128 * p + 128] = l
        for t in range(6):
            res = dot_left((l2_ref[0], l2_ref[1]), (high_ref[t], low_ref[t]), NT)
            for p in range(2):
                out_ref[pl.ds(12 * j + 6 * p + t, 128, stride=PITCH), :] = res[128 * p:128 * p + 128]
        return 0

    lax.fori_loop(0, 3, body, 0)


def far_field_kernel(in_ref, ph_ref, l_ref, r_ref, r2_ref, tw_ref, out_ref, y_ref, w_ref, high_ref, low_ref):
    def body(g, _):
        over_senders(in_ref, g, (0, 12, 24), (l_ref[0], l_ref[1]), y_ref)
        for u in range(0, 128, 16):
            z = []
            for t in range(3):
                lanes = slice(128 * t, 128 * t + 128)
                w = (tw_ref[0, t, u:u + 16, :], tw_ref[1, t, u:u + 16, :])
                z.append(turn((y_ref[u:u + 16, lanes], y_ref[128 + u:144 + u, lanes]), w))
            z = dft3(*z)
            for t in range(3):
                for p in range(2):
                    h, l = split(z[t][p])
                    high_ref[t, u:u + 16, 128 * p:128 * p + 128] = h
                    low_ref[t, u:u + 16, 128 * p:128 * p + 128] = l
        for t in range(3):
            z = dot_right((high_ref[t], low_ref[t]), (r_ref[0, t], r_ref[1, t]), NN)
            z = turn((z[:, :128], z[:, 128:]), (ph_ref[0, t, g], ph_ref[1, t, g]))
            w_ref[t] = dot_right(split(jnp.concatenate(z, 1)), (r2_ref[0, t], r2_ref[1, t]), NN)
        for u in range(0, 128, 16):
            z = dft3(*[(w_ref[t, u:u + 16, :128], w_ref[t, u:u + 16, 128:]) for t in range(3)])
            for t in range(3):
                q = turn(z[t], (tw_ref[0, t, u:u + 16, :], tw_ref[1, t, u:u + 16, :]))
                for p in range(2):
                    y_ref[128 * p + u:128 * p + u + 16, 128 * t:128 * t + 128] = q[p]
        res = dot_left((l_ref[0], l_ref[1]), split(y_ref[...]), NN)
        for t in range(3):
            for p in range(2):
                out_ref[pl.ds(12 * t + 6 * p + g, 128, stride=PITCH), :] = res[128 * p:128 * p + 128, 128 * t:128 * t + 128]
        return 0

    lax.fori_loop(0, 6, body, 0)


def leave_kernel(in_ref, l_ref, m_ref, tw_ref, out_ref, y_ref, high_ref, low_ref):
    def body(j, _):
        rows_first(in_ref, j, l_ref, tw_ref, y_ref, high_ref, low_ref)
        for t in range(6):
            z = dot_left((m_ref[0, t], m_ref[1, t]), (high_ref[t], low_ref[t]), NT)
            for p in range(2):
                rows = pl.ds(pl.multiple_of(48 * p + 16 * j, 16), 16)
                out_ref[:, rows, 128 * t:128 * t + 128] = z[128 * p:128 * p + 128].reshape(8, 16, 128)
        return 0

    lax.fori_loop(0, 3, body, 0)


def aperture_kernel(pin_ref, hx_ref, hy_ref, out_ref, t_ref):
    for v in range(48):
        t_ref[:, 128 * v:128 * v + 128] = pin_ref[128 * v:128 * v + 128, :].astype(F32).T
    for t in range(3):
        for g in range(6):
            block = jnp.concatenate([t_ref[8 * g:8 * g + 8, 128 * (t + 3 * k):128 * (t + 3 * k) + 128] for k in range(16)], 0)
            block = block.T
            h = turn((hx_ref[0, t], hx_ref[1, t]), (hy_ref[0, g:g + 1, :], hy_ref[1, g:g + 1, :]))
            for p in range(2):
                out_ref[p, t, g] = block * h[p]


def call(kernel, outs, args, scratch=(), flops=0):
    size = sum(a.size * a.dtype.itemsize for a in args)
    return pl.pallas_call(
        kernel,
        out_shape=outs,
        scratch_shapes=list(scratch),
        compiler_params=pltpu.CompilerParams(vmem_limit_bytes=VMEM_LIMIT),
        cost_estimate=pl.CostEstimate(flops=flops, bytes_accessed=size + 2_400_000, transcendentals=0),
    )(*args)


def shape(*dims):
    return jax.ShapeDtypeStruct(dims, F32)


def exchange(x, axis):
    return lax.all_to_all(x, axis, split_axis=0, concat_axis=0, tiled=True)


def per_device(field_real, field_imag, kerr_map, pinhole):
    tb = {k: jnp.asarray(v) for k, v in TABLES.items()}
    row_at, col_at = lax.axis_index("rows"), lax.axis_index("cols")
    me = lax.axis_index(("rows", "cols"))
    both = ("rows", "cols")
    ints = lambda n: jnp.arange(n, dtype=jnp.int32)
    kerr_rows = exchange(kerr_map.reshape(8, 48, 768), "cols")
    ax0 = chirp_angle(row_at * 384 + ints(384)).reshape(384, 1)
    ay0 = chirp_angle(col_at * 768 + ints(768)).reshape(1, 768)
    sent, phase_one = call(
        enter_kernel, (shape(16, 96, 384), shape(384, 768)), (field_real, field_imag, kerr_map, ax0, ay0)
    )
    cols = exchange(sent, "rows")
    sent = call(
        columns_kernel, shape(DEV * PITCH, 128), (cols, tb["d384"], tb["tw1"]),
        (pltpu.VMEM((768, 768), BF16), pltpu.VMEM((768, 768), BF16)),
    )
    rows = exchange(sent.reshape(DEV, PITCH, 128), both).reshape(DEV * PITCH, 128)
    ax1 = chirp_angle(me * 48 + 16 * ints(3)[:, None, None] + ints(16)[None, None, :])
    ax1 = jnp.broadcast_to(ax1, (3, 8, 16)).reshape(384, 1)
    pair6 = (pltpu.VMEM((6, 128, 256), BF16), pltpu.VMEM((6, 128, 256), BF16))
    sent, phase_two = call(
        rows_kernel, (shape(DEV * PITCH, 128), shape(8, 48, 768)),
        (rows, kerr_rows, ax1, tb["chirp_y"], tb["l_mixed"], tb["m_first"], tb["m_second"], tb["l_plain"],
         tb["tw_u_a"], tb["tw_a_u"]),
        (pltpu.VMEM((256, 768), F32), pltpu.VMEM((6, 256, 128), F32)) + pair6,
    )
    far = exchange(sent.reshape(DEV, PITCH, 128), both).reshape(DEV * PITCH, 128)
    ky = me * 48 + 8 * ints(6)[:, None, None] + ints(8)[None, None, :]
    ky_angle = -chirp_angle(jnp.broadcast_to(ky, (6, 16, 8)).reshape(6, 128))
    h_y = jnp.stack([jnp.cos(ky_angle), jnp.sin(ky_angle)])
    aperture = call(
        aperture_kernel, shape(2, 3, 6, 128, 128), (pinhole, tb["h_x"], h_y), (pltpu.VMEM((48, N), F32),)
    )
    pair3 = (pltpu.VMEM((3, 128, 256), BF16), pltpu.VMEM((3, 128, 256), BF16))
    sent = call(
        far_field_kernel, shape(DEV * PITCH, 128),
        (far, aperture, tb["l_plain"], tb["r_in"], tb["r_out"], tb["tw_u_rho"]),
        (pltpu.VMEM((256, 384), F32), pltpu.VMEM((3, 128, 256), F32)) + pair3,
    )
    phase_back = exchange(phase_two, "cols").reshape(384, 768)
    b_integral = phase_one + phase_back
    near = exchange(sent.reshape(DEV, PITCH, 128), both).reshape(DEV * PITCH, 128)
    sent = call(
        leave_kernel, shape(8, 96, 768), (near, tb["l_plain"], tb["m_first"], tb["tw_u_a"]),
        (pltpu.VMEM((256, 768), F32),) + pair6,
    )
    out = exchange(sent, "cols")
    return (out[:, :48].reshape(384, 768), out[:, 48:].reshape(384, 768), b_integral)


def solution(mesh):
    tiles = P("rows", "cols")
    return jax.shard_map(
        per_device,
        mesh=mesh,
        in_specs=(tiles, tiles, tiles, P(None, ("rows", "cols"))),
        out_specs=(tiles, tiles, tiles),
        check_vma=False,
    )
```

```python
import math

import jax
import jax.numpy as jnp
import ml_dtypes
import numpy as np
from jax import lax
from jax.experimental import pallas as pl
from jax.experimental.pallas import tpu as pltpu
from jax.sharding import PartitionSpec as P

N = 6144
DEV = 128
PITCH = 40
EDGE = 44
KEPT = 32
MOVED = (np.arange(40), np.arange(88, 128), np.array([40, 41, 42, 43, 84, 85, 86, 87]))
F32 = jnp.float32
BF16 = jnp.bfloat16
NT = (((1,), (1,)), ((), ()))
NN = (((1,), (0,)), ((), ()))


def root(period, product):
    return np.exp(-2j * np.pi * (np.asarray(product) % period) / period)


def real_form(matrix):
    return np.block([[matrix.real, -matrix.imag], [matrix.imag, matrix.real]])


def halves(matrix):
    high = matrix.astype(np.float32).astype(ml_dtypes.bfloat16)
    low = (matrix - high.astype(np.float64)).astype(ml_dtypes.bfloat16)
    return np.stack([high, low])


def planes(table):
    return np.stack([table.real, table.imag]).astype(np.float32)


def make_tables():
    t = {}
    r128 = np.arange(128)
    n1_of_src = 16 * (r128 % 8) + r128 // 8
    s128 = 1 / math.sqrt(128)
    s48 = 1 / math.sqrt(48)
    t["tw_rho_j"] = planes(root(N, np.arange(48)[:, None] * r128[None, :]).reshape(48, 1, 128) * s48)
    t["l_mixed"] = halves(real_form(root(128, r128[:, None] * n1_of_src[None, :]) * s128))
    plain = root(128, r128[:, None] * r128[None, :]) * s128
    t["l_plain"] = halves(real_form(plain))
    outer = (r128 >= EDGE) & (r128 < DEV - EDGE)
    t["l_kept"] = halves(real_form(np.where(outer[None, :], 0, plain)))
    t["l_moved"] = halves(real_form(plain[:, np.concatenate(MOVED)]))
    lane_q, lane_8 = r128 // 8, r128 % 8
    row_8, row_q = r128 // 16, r128 % 16
    same = (row_q[:, None] == lane_q[None, :]).astype(np.float64)
    g6 = np.arange(6)[:, None, None]
    first = same * root(48, lane_8[None, None, :] * g6 + 6 * row_8[None, :, None] * lane_8[None, None, :]) * s48
    t["m_first"] = np.stack([halves(real_form(m)) for m in first], 1)
    second = same.T * root(48, g6 * lane_8[None, :, None] + 6 * row_8[None, None, :] * lane_8[None, :, None]) * s48
    t["m_second"] = np.stack([halves(real_form(m)) for m in second], 1)
    a = lane_8[None, :] + 8 * np.arange(6)[:, None]
    tw = root(N, r128[None, :, None] * a[:, None, :])
    t["tw_u_a"] = planes(tw)
    t["tw_a_u"] = planes(tw.transpose(0, 2, 1))
    keep = (lane_8[:, None] == lane_8[None, :]).astype(np.float64)
    v3 = np.arange(3)[:, None, None]
    into = keep * root(48, lane_q[None, :, None] * v3 + 3 * lane_q[None, :, None] * lane_q[None, None, :]) * s48
    t["r_in"] = np.stack([halves(real_form(m.T).T) for m in into], 1)
    back = keep * root(48, lane_q[None, None, :] * v3 + 3 * lane_q[None, :, None] * lane_q[None, None, :]) * s48
    t["r_out"] = np.stack([halves(real_form(m.T).T) for m in back], 1)
    rho = lane_q[None, :] + 16 * np.arange(3)[:, None]
    t["tw_u_rho"] = planes(root(N, r128[None, :, None] * rho[:, None, :]))
    kx = r128[None, :, None] + 128 * (np.arange(3)[:, None, None] + 3 * lane_q[None, None, :])
    t["h_x"] = planes(root(2 * N, kx * kx))
    y = r128[None, None, :] + 128 * (np.arange(6)[:, None, None] + 6 * row_8[None, :, None])
    t["chirp_y"] = (math.pi / N * ((y * y + N) % (2 * N) - N)).astype(np.float32)
    return t


TABLES = make_tables()


def chirp_angle(index):
    return math.pi / N * ((index * index + N) % (2 * N) - N).astype(F32)


def sin_cos(angle):
    turns = jnp.floor(angle * (2.0 / math.pi) + 0.5)
    r = angle - turns * 1.5703125
    r = r - turns * 4.837512969970703e-4
    r = r - turns * 7.549789948768648e-8
    quarter = turns.astype(jnp.int32)
    r2 = r * r
    sine = r + r * r2 * (-1.6666654611e-1 + r2 * (8.3321608736e-3 + r2 * -1.9515295891e-4))
    cosine = 1.0 - 0.5 * r2 + r2 * r2 * (4.166664568298827e-2 + r2 * (-1.388731625493765e-3 + r2 * 2.443315711809948e-5))
    odd = (quarter & 1) == 1
    s = jnp.where(odd, cosine, sine)
    c = jnp.where(odd, sine, cosine)
    s = jnp.where((quarter & 2) == 2, -s, s)
    c = jnp.where(((quarter + 1) & 2) == 2, -c, c)
    return s, c


def split(x):
    high = x.astype(BF16)
    return high, (x - high.astype(F32)).astype(BF16)


def mm(a, b, dims):
    return lax.dot_general(a, b, dims, preferred_element_type=F32)


def dot_left(table, data, dims):
    left = jnp.concatenate([table[0], table[0], table[1]], 1)
    return mm(left, jnp.concatenate([data[0], data[1], data[0]], dims[0][1][0]), dims)


def dot_right(data, table, dims):
    right = jnp.concatenate([table[0], table[0], table[1]], 0)
    return mm(jnp.concatenate([data[0], data[1], data[0]], 1), right, dims)


def turn(z, w):
    return (z[0] * w[0] - z[1] * w[1], z[0] * w[1] + z[1] * w[0])


def add(a, b):
    return (a[0] + b[0], a[1] + b[1])


def sub(a, b):
    return (a[0] - b[0], a[1] - b[1])


def minus_i(a):
    return (a[1], -a[0])


def by_const(a, w):
    return (a[0] * w.real - a[1] * w.imag, a[0] * w.imag + a[1] * w.real)


def dft2(a, b):
    return add(a, b), sub(a, b)


def dft3(a, b, c):
    s = add(b, c)
    d = sub(b, c)
    h = math.sqrt(0.75)
    m = (a[0] - 0.5 * s[0], a[1] - 0.5 * s[1])
    e = (h * d[1], -h * d[0])
    return add(a, s), add(m, e), sub(m, e)


def dft4(a, b, c, d):
    p, q = dft2(a, c)
    r, s = dft2(b, d)
    s = minus_i(s)
    return add(p, r), add(q, s), sub(p, r), sub(q, s)


def dft6(z):
    even = dft3(z[0], z[2], z[4])
    odd = dft3(z[3], z[5], z[1])
    out = [None] * 6
    for k in range(6):
        f = add if k % 2 == 0 else sub
        out[k] = f(even[k % 3], odd[k % 3])
    return out


def dft16(z):
    cols = [dft4(z[i], z[i + 4], z[i + 8], z[i + 12]) for i in range(4)]
    out = [None] * 16
    for k1 in range(4):
        row = []
        for i in range(4):
            e = (i * k1) % 16
            row.append(cols[i][k1] if e == 0 else by_const(cols[i][k1], np.exp(-2j * np.pi * e / 16)))
        res = dft4(*row)
        for k2 in range(4):
            out[k1 + 4 * k2] = res[k2]
    return out


def enter_kernel(re_ref, im_ref, kerr_ref, ax_ref, ay_ref, out_ref, phase_ref):
    for lb in range(6):
        cols = slice(128 * lb, 128 * lb + 128)
        re, im = re_ref[:, cols], im_ref[:, cols]
        phase = kerr_ref[:, cols] * (re * re + im * im)
        phase_ref[:, cols] = phase
        s, c = sin_cos(phase + (ax_ref[...] + ay_ref[:, cols]))
        both = turn((re, im), (c, s))
        for p in range(2):
            turned = both[p].T
            for i in range(8):
                l = 128 * lb + 16 * i
                out_ref[l // 48, pl.ds(48 * p + l % 48, 16), :] = turned[16 * i:16 * i + 16]


def columns_kernel(in_ref, l_ref, tw_ref, out_ref, z_ref, high_ref, low_ref):
    def body(lh, _):
        low = pl.ds(pl.multiple_of(8 * lh, 8), 8)
        high = pl.ds(pl.multiple_of(48 + 8 * lh, 8), 8)
        for j3 in range(3):
            lanes = slice(128 * j3, 128 * j3 + 128)
            at = [(n + 5 * j3) % 16 for n in range(16)]
            z = dft16([(in_ref[r, low, lanes], in_ref[r, high, lanes]) for r in at])
            for k in range(16):
                z_ref[j3, k, 0] = z[k][0]
                z_ref[j3, k, 1] = z[k][1]
        for k in range(0, 16, 2):
            found = {}
            for m in (k, k + 1):
                z = dft3(*[(z_ref[j3, m, 0], z_ref[j3, m, 1]) for j3 in range(3)])
                for k3 in range(3):
                    rho = next(r for r in range(48) if r % 16 == m and r % 3 == k3)
                    found[rho] = turn(z[k3], (tw_ref[0, rho], tw_ref[1, rho]))
            for rho in sorted(found):
                if rho % 2 == 0:
                    rows = slice(8 * rho, 8 * rho + 16)
                    for p in range(2):
                        h, l = split(jnp.concatenate([found[rho][p], found[rho + 1][p]], 0))
                        high_ref[rows, 128 * p:128 * p + 128] = h
                        low_ref[rows, 128 * p:128 * p + 128] = l
        res = dot_left((l_ref[0], l_ref[1]), (high_ref[...], low_ref[...]), NT)
        for j in range(3):
            for p in range(2):
                out_ref[pl.ds(12 * j + 6 * p + lh, 128, stride=PITCH), :] = res[128 * p:128 * p + 128, 128 * j:128 * j + 128]
        return 0

    lax.fori_loop(0, 6, body, 0)


def gather_rows(in_ref, row, pitch, count=128, first=0):
    return in_ref[pl.ds(first * pitch + row, count, stride=pitch), :]


def over_senders(in_ref, rows, pitch, table, out_ref):
    data = jnp.concatenate([jnp.concatenate([gather_rows(in_ref, r, pitch) for r in pair], 0) for pair in rows], 1)
    out_ref[:, :data.shape[1]] = dot_left(table, split(data), NN)


def after_senders(tw_ref, y_ref, high_ref, low_ref):
    for u in range(0, 128, 16):
        z = []
        for t in range(6):
            lanes = slice(128 * t, 128 * t + 128)
            w = (tw_ref[0, t, u:u + 16, :], tw_ref[1, t, u:u + 16, :])
            z.append(turn((y_ref[u:u + 16, lanes], y_ref[128 + u:144 + u, lanes]), w))
        z = dft6(z)
        for t in range(6):
            for p in range(2):
                h, l = split(z[t][p])
                high_ref[t, u:u + 16, 128 * p:128 * p + 128] = h
                low_ref[t, u:u + 16, 128 * p:128 * p + 128] = l


def rows_kernel(in_ref, kerr_ref, ax_ref, ay_ref, l_ref, m_ref, m2_ref, l2_ref, tw_ref, tw2_ref,
                out_ref, phase_ref, y_ref, w_ref, high_ref, low_ref):
    def body(j, _):
        over_senders(in_ref, [(12 * j + t, 12 * j + 6 + t) for t in range(6)], PITCH, (l_ref[0], l_ref[1]), y_ref)
        after_senders(tw_ref, y_ref, high_ref, low_ref)
        rows = pl.ds(pl.multiple_of(16 * j, 16), 16)
        ax = ax_ref[pl.ds(pl.multiple_of(128 * j, 128), 128), :]
        for t in range(6):
            z = dot_left((m_ref[0, t], m_ref[1, t]), (high_ref[t], low_ref[t]), NT)
            re, im = z[:128], z[128:]
            lanes = slice(128 * t, 128 * t + 128)
            phase = kerr_ref[:, rows, lanes].reshape(128, 128) * (re * re + im * im)
            phase_ref[:, rows, lanes] = phase.reshape(8, 16, 128)
            s, c = sin_cos(phase + (ax + ay_ref[t]))
            both = jnp.concatenate(turn((im, -re), (c, s)), 0)
            w_ref[t] = dot_left((m2_ref[0, t], m2_ref[1, t]), split(both), NN)
        for r in range(0, 128, 16):
            z = dft6([(w_ref[t, r:r + 16, :], w_ref[t, 128 + r:144 + r, :]) for t in range(6)])
            for t in range(6):
                q = turn(z[t], (tw2_ref[0, t, r:r + 16, :], tw2_ref[1, t, r:r + 16, :]))
                for p in range(2):
                    h, l = split(q[p])
                    high_ref[t, r:r + 16, 128 * p:128 * p + 128] = h
                    low_ref[t, r:r + 16, 128 * p:128 * p + 128] = l
        for t in range(6):
            res = dot_left((l2_ref[0], l2_ref[1]), (high_ref[t], low_ref[t]), NT)
            for p in range(2):
                row = 2 * j + p
                if t < 5:
                    out_ref[pl.ds(6 * t + row, 128, stride=KEPT), :] = res[128 * p:128 * p + 128]
                else:
                    y_ref[128 * p:128 * p + 128, :128] = res[128 * p:128 * p + 128]
                    for slot in range(2):
                        b = 128 * p + int(MOVED[slot][0])
                        out_ref[pl.ds(EDGE * KEPT + 6 * slot + row, 40, stride=KEPT), :] = y_ref[b:b + 40, :128]
                    out_ref[pl.ds(EDGE * KEPT + 12 + row, 4, stride=KEPT), :] = y_ref[128 * p + 40:128 * p + 44, :128]
                    out_ref[pl.ds((EDGE + 4) * KEPT + 12 + row, 4, stride=KEPT), :] = y_ref[128 * p + 84:128 * p + 88, :128]
        return 0

    lax.fori_loop(0, 3, body, 0)


def far_field_kernel(in_ref, ph_ref, l_ref, r_ref, r2_ref, tw_ref, out_ref, y_ref, w_ref, high_ref, low_ref):
    def body(g, _):
        over_senders(in_ref, [(6 * g + 2 * j, 6 * g + 2 * j + 1) for j in range(3)], KEPT, (l_ref[0], l_ref[1]), y_ref)
        for u in range(0, 128, 16):
            z = []
            for t in range(3):
                lanes = slice(128 * t, 128 * t + 128)
                w = (tw_ref[0, t, u:u + 16, :], tw_ref[1, t, u:u + 16, :])
                z.append(turn((y_ref[u:u + 16, lanes], y_ref[128 + u:144 + u, lanes]), w))
            z = dft3(*z)
            for t in range(3):
                for p in range(2):
                    h, l = split(z[t][p])
                    high_ref[t, u:u + 16, 128 * p:128 * p + 128] = h
                    low_ref[t, u:u + 16, 128 * p:128 * p + 128] = l
        for t in range(3):
            z = dot_right((high_ref[t], low_ref[t]), (r_ref[0, t], r_ref[1, t]), NN)
            z = turn((z[:, :128], z[:, 128:]), (ph_ref[0, t, g], ph_ref[1, t, g]))
            w_ref[t] = dot_right(split(jnp.concatenate(z, 1)), (r2_ref[0, t], r2_ref[1, t]), NN)
        for u in range(0, 128, 16):
            z = dft3(*[(w_ref[t, u:u + 16, :128], w_ref[t, u:u + 16, 128:]) for t in range(3)])
            for t in range(3):
                q = turn(z[t], (tw_ref[0, t, u:u + 16, :], tw_ref[1, t, u:u + 16, :]))
                for p in range(2):
                    y_ref[128 * p + u:128 * p + u + 16, 128 * t:128 * t + 128] = q[p]
        res = dot_left((l_ref[0], l_ref[1]), split(y_ref[...]), NN)
        for t in range(3):
            for p in range(2):
                out_ref[pl.ds(6 * g + 2 * t + p, 128, stride=KEPT), :] = res[128 * p:128 * p + 128, 128 * t:128 * t + 128]
        return 0

    lax.fori_loop(0, 5, body, 0)


def leave_kernel(in_ref, l_ref, lm_ref, m_ref, tw_ref, out_ref, y_ref, high_ref, low_ref):
    def body(j, _):
        row = 2 * j
        over_senders(in_ref, [(6 * t + row, 6 * t + row + 1) for t in range(5)], KEPT, (l_ref[0], l_ref[1]), y_ref)
        moved = [gather_rows(in_ref, 6 * slot + row + p, KEPT, len(MOVED[slot]), EDGE) for p in range(2) for slot in range(3)]
        y_ref[:, 640:] = dot_left((lm_ref[0], lm_ref[1]), split(jnp.concatenate(moved, 0)), NN)
        after_senders(tw_ref, y_ref, high_ref, low_ref)
        for t in range(6):
            z = dot_left((m_ref[0, t], m_ref[1, t]), (high_ref[t], low_ref[t]), NT)
            for p in range(2):
                rows = pl.ds(pl.multiple_of(48 * p + 16 * j, 16), 16)
                out_ref[:, rows, 128 * t:128 * t + 128] = z[128 * p:128 * p + 128].reshape(8, 16, 128)
        return 0

    lax.fori_loop(0, 3, body, 0)


def aperture_kernel(at_ref, pin_ref, m0_ref, m1_ref, m2_ref, hx_ref, hy_ref, out_ref):
    outer = at_ref[0]
    for g in range(5):
        if g < 3:
            moved = (m0_ref, m1_ref, m2_ref)[g]
            rows = jnp.where(outer > g, moved[...], pin_ref[8 * g:8 * g + 8, :]).astype(F32)
        else:
            rows = pin_ref[8 * g:8 * g + 8, :].astype(F32)
        for t in range(3):
            block = jnp.concatenate([rows[:, 128 * (t + 3 * k):128 * (t + 3 * k) + 128] for k in range(16)], 0)
            block = block.T
            h = turn((hx_ref[0, t], hx_ref[1, t]), (hy_ref[0, g:g + 1, :], hy_ref[1, g:g + 1, :]))
            for p in range(2):
                out_ref[p, t, g] = block * h[p]


def nbytes(a):
    return math.prod(a.shape) * jnp.dtype(a.dtype).itemsize


def call(kernel, outs, args, scratch=(), spec=None):
    size = sum(nbytes(a) for a in args) + sum(nbytes(o) for o in jax.tree.leaves(outs))
    held = sum(math.prod(r.shape) * jnp.dtype(r.dtype).itemsize for r in scratch)
    return pl.pallas_call(
        kernel,
        out_shape=outs,
        scratch_shapes=list(scratch),
        compiler_params=pltpu.CompilerParams(vmem_limit_bytes=size + held + 8 * 2**20),
        cost_estimate=pl.CostEstimate(flops=0, bytes_accessed=size, transcendentals=0),
        **(spec or {}),
    )(*args)


def shape(*dims):
    return jax.ShapeDtypeStruct(dims, F32)


def exchange(x, axis):
    return lax.all_to_all(x, axis, split_axis=0, concat_axis=0, tiled=True)


def make_aperture(pinhole, me, tb):
    turned = pinhole.T
    moves = [[(int(b), EDGE + i) for i, b in enumerate(m)] for m in MOVED]
    moved = [lax.ppermute(turned[40:48], ("rows", "cols"), pairs) for pairs in moves]
    place = me - EDGE
    inside = (place >= 0) & (place < DEV - 2 * EDGE)
    taken = jnp.where(inside, 2 + (place < len(MOVED[2])).astype(jnp.int32), 0)
    ky = 48 * me + 8 * jnp.arange(6, dtype=jnp.int32)
    for slot, m in enumerate(MOVED):
        source = jnp.asarray(m, jnp.int32)[jnp.clip(place, 0, len(m) - 1)]
        ky = ky.at[slot].set(jnp.where(taken > slot, 48 * source + 40, ky[slot]))
    ky = ky[:, None, None] + jnp.arange(8, dtype=jnp.int32)[None, None, :]
    angle = -chirp_angle(jnp.broadcast_to(ky, (6, 16, 8)).reshape(6, 128))
    h_y = jnp.stack([jnp.cos(angle), jnp.sin(angle)])
    whole = pl.BlockSpec(memory_space=pltpu.VMEM)
    return call(
        aperture_kernel, shape(2, 3, 5, 128, 128), (taken.reshape(1), turned, *moved, tb["h_x"], h_y),
        spec=dict(in_specs=[pl.BlockSpec(memory_space=pltpu.SMEM)] + [whole] * 6),
    )


def per_device(field_real, field_imag, kerr_map, pinhole):
    tb = {k: jnp.asarray(v) for k, v in TABLES.items()}
    row_at, col_at = lax.axis_index("rows"), lax.axis_index("cols")
    me = lax.axis_index(("rows", "cols"))
    both = ("rows", "cols")
    ints = lambda n: jnp.arange(n, dtype=jnp.int32)
    kerr_rows = exchange(kerr_map.reshape(8, 48, 768), "cols")
    ax0 = chirp_angle(row_at * 384 + ints(384)).reshape(384, 1)
    ay0 = chirp_angle(col_at * 768 + ints(768)).reshape(1, 768)
    strip = pl.BlockSpec((128, 768), lambda i: (i, 0))
    enter = dict(
        grid=(3,),
        in_specs=[strip, strip, strip, pl.BlockSpec((128, 1), lambda i: (i, 0)), pl.BlockSpec((1, 768), lambda i: (0, 0))],
        out_specs=(pl.BlockSpec((16, 96, 128), lambda i: (0, 0, i)), strip),
    )
    sent, phase_one = call(
        enter_kernel, (shape(16, 96, 384), shape(384, 768)), (field_real, field_imag, kerr_map, ax0, ay0), spec=enter
    )
    cols = exchange(sent, "rows")
    sent = call(
        columns_kernel, shape(DEV * PITCH, 128), (cols, tb["l_plain"], tb["tw_rho_j"]),
        (pltpu.VMEM((3, 16, 2, 8, 128), F32), pltpu.VMEM((384, 256), BF16), pltpu.VMEM((384, 256), BF16)),
    )
    rows = exchange(sent.reshape(DEV, PITCH, 128), both).reshape(DEV * PITCH, 128)
    ax1 = chirp_angle(me * 48 + 16 * ints(3)[:, None, None] + ints(16)[None, None, :])
    ax1 = jnp.broadcast_to(ax1, (3, 8, 16)).reshape(384, 1)
    pair6 = (pltpu.VMEM((6, 128, 256), BF16), pltpu.VMEM((6, 128, 256), BF16))
    sent, phase_two = call(
        rows_kernel, (shape(DEV * KEPT, 128), shape(8, 48, 768)),
        (rows, kerr_rows, ax1, tb["chirp_y"], tb["l_mixed"], tb["m_first"], tb["m_second"], tb["l_plain"],
         tb["tw_u_a"], tb["tw_a_u"]),
        (pltpu.VMEM((256, 768), F32), pltpu.VMEM((6, 256, 128), F32)) + pair6,
    )
    far = exchange(sent.reshape(DEV, KEPT, 128), both).reshape(DEV * KEPT, 128)
    far, phase_two = lax.optimization_barrier((far, phase_two))
    phase_back = exchange(phase_two, "cols").reshape(384, 768)
    aperture = make_aperture(pinhole, me, tb)
    pair3 = (pltpu.VMEM((3, 128, 256), BF16), pltpu.VMEM((3, 128, 256), BF16))
    sent = call(
        far_field_kernel, shape(DEV * KEPT, 128),
        (far, aperture, tb["l_plain"], tb["r_in"], tb["r_out"], tb["tw_u_rho"]),
        (pltpu.VMEM((256, 384), F32), pltpu.VMEM((3, 128, 256), F32)) + pair3,
    )
    sent, phase_back = lax.optimization_barrier((sent, phase_back))
    near = exchange(sent.reshape(DEV, KEPT, 128), both).reshape(DEV * KEPT, 128)
    b_integral = phase_one + phase_back
    sent = call(
        leave_kernel, shape(8, 96, 768), (near, tb["l_kept"], tb["l_moved"], tb["m_first"], tb["tw_u_a"]),
        (pltpu.VMEM((256, 768), F32),) + pair6,
    )
    out = exchange(sent, "cols")
    return (out[:, :48].reshape(384, 768), out[:, 48:].reshape(384, 768), b_integral)


def solution(mesh):
    tiles = P("rows", "cols")
    return jax.shard_map(
        per_device,
        mesh=mesh,
        in_specs=(tiles, tiles, tiles, P(None, ("rows", "cols"))),
        out_specs=(tiles, tiles, tiles),
        check_vma=False,
    )
```

```python
import math

import jax
import jax.numpy as jnp
import ml_dtypes
import numpy as np
from jax import lax
from jax.experimental import pallas as pl
from jax.experimental.pallas import tpu as pltpu
from jax.sharding import PartitionSpec as P

N = 6144
DEV = 128
PITCH = 40
EDGE = 44
KEPT = 32
MOVED = (np.arange(40), np.arange(88, 128), np.array([40, 41, 42, 43, 84, 85, 86, 87]))
F32 = jnp.float32
BF16 = jnp.bfloat16
NT = (((1,), (1,)), ((), ()))
NN = (((1,), (0,)), ((), ()))


def root(period, product):
    return np.exp(-2j * np.pi * (np.asarray(product) % period) / period)


def real_form(matrix):
    return np.block([[matrix.real, -matrix.imag], [matrix.imag, matrix.real]])


def halves(matrix):
    high = matrix.astype(np.float32).astype(ml_dtypes.bfloat16)
    low = (matrix - high.astype(np.float64)).astype(ml_dtypes.bfloat16)
    return np.stack([high, low])


def planes(table):
    return np.stack([table.real, table.imag]).astype(np.float32)


def make_tables():
    t = {}
    r128 = np.arange(128)
    n1_of_src = 16 * (r128 % 8) + r128 // 8
    s128 = 1 / math.sqrt(128)
    s48 = 1 / math.sqrt(48)
    t["tw_rho_j"] = planes(root(N, np.arange(48)[:, None] * r128[None, :]).reshape(48, 1, 128) * s48)
    t["l_mixed"] = halves(real_form(root(128, r128[:, None] * n1_of_src[None, :]) * s128))
    plain = root(128, r128[:, None] * r128[None, :]) * s128
    t["l_plain"] = halves(real_form(plain))
    outer = (r128 >= EDGE) & (r128 < DEV - EDGE)
    t["l_kept"] = halves(real_form(np.where(outer[None, :], 0, plain)))
    t["l_moved"] = halves(real_form(plain[:, np.concatenate(MOVED)]))
    lane_q, lane_8 = r128 // 8, r128 % 8
    row_8, row_q = r128 // 16, r128 % 16
    same = (row_q[:, None] == lane_q[None, :]).astype(np.float64)
    eight = same * root(8, row_8[:, None] * lane_8[None, :]) * s48
    t["m_first"] = halves(real_form(eight))
    t["m_second"] = halves(real_form(eight.T))
    six = np.arange(6)
    t["v_6"] = planes(root(48, six[:, None, None] * lane_8[None, None, :]))
    t["v_6_rows"] = planes(root(48, six[:, None, None] * (np.arange(16) % 8)[None, :, None]) * np.ones((1, 1, 128)))
    a = lane_8[None, :] + 8 * six[:, None]
    t["tw_u_a"] = planes(root(N, r128[None, :, None] * a[:, None, :]))
    a = np.arange(16)[None, :] % 8 + 8 * six[:, None]
    t["tw_a_u"] = planes(root(N, r128[None, None, :] * a[:, :, None]))
    keep = (lane_8[:, None] == lane_8[None, :]).astype(np.float64)
    sixteen = keep * root(16, lane_q[:, None] * lane_q[None, :]) * s48
    t["r_16"] = halves(real_form(sixteen).T)
    t["v_3"] = planes(root(48, np.arange(3)[:, None, None] * lane_q[None, None, :]))
    rho = lane_q[None, :] + 16 * np.arange(3)[:, None]
    t["tw_u_rho"] = planes(root(N, r128[None, :, None] * rho[:, None, :]))
    kx = r128[None, :, None] + 128 * (np.arange(3)[:, None, None] + 3 * lane_q[None, None, :])
    t["h_x"] = planes(root(2 * N, kx * kx))
    y = r128[None, None, :] + 128 * (six[:, None, None] + 6 * np.arange(8)[None, :, None])
    t["chirp_y"] = (math.pi / N * ((y * y + N) % (2 * N) - N)).astype(np.float32)
    taken = np.zeros(DEV, np.int32)
    ky = 48 * np.arange(DEV)[:, None] + 8 * np.arange(6)[None, :]
    for slot, m in enumerate(MOVED):
        for place, b in enumerate(m):
            taken[EDGE + place] = slot + 1
            ky[EDGE + place, slot] = 48 * b + 40
    t["taken"] = taken
    ky = ky[:, :, None] + lane_8[None, None, :]
    t["h_y"] = planes(root(2 * N, ky * ky)).transpose(1, 0, 2, 3)
    return t


TABLES = make_tables()


def chirp_angle(index):
    square = index * index
    turns = (square.astype(F32) * (0.5 / N)).astype(jnp.int32)
    return (math.pi / N) * (square - 2 * N * turns).astype(F32)


def sin_cos(angle):
    turns = jnp.floor(angle * (2.0 / math.pi) + 0.5)
    r = angle - turns * 1.5703125
    r = r - turns * 4.837512969970703e-4
    r = r - turns * 7.549789948768648e-8
    quarter = turns.astype(jnp.int32)
    r2 = r * r
    sine = r + r * r2 * (-1.6666654611e-1 + r2 * (8.3321608736e-3 + r2 * -1.9515295891e-4))
    cosine = 1.0 - 0.5 * r2 + r2 * r2 * (4.166664568298827e-2 + r2 * (-1.388731625493765e-3 + r2 * 2.443315711809948e-5))
    odd = (quarter & 1) == 1
    s = jnp.where(odd, cosine, sine)
    c = jnp.where(odd, sine, cosine)
    s = jnp.where((quarter & 2) == 2, -s, s)
    c = jnp.where(((quarter + 1) & 2) == 2, -c, c)
    return s, c


def split(x):
    high = x.astype(BF16)
    return high, (x - high.astype(F32)).astype(BF16)


def mm(a, b, dims):
    return lax.dot_general(a, b, dims, preferred_element_type=F32)


def dot_left(table, data, dims):
    left = jnp.concatenate([table[0], table[0], table[1]], 1)
    return mm(left, jnp.concatenate([data[0], data[1], data[0]], dims[0][1][0]), dims)


def dot_right(data, table, dims):
    right = jnp.concatenate([table[0], table[0], table[1]], 0)
    return mm(jnp.concatenate([data[0], data[1], data[0]], 1), right, dims)


def turn(z, w):
    return (z[0] * w[0] - z[1] * w[1], z[0] * w[1] + z[1] * w[0])


def add(a, b):
    return (a[0] + b[0], a[1] + b[1])


def sub(a, b):
    return (a[0] - b[0], a[1] - b[1])


def minus_i(a):
    return (a[1], -a[0])


def by_const(a, w):
    return (a[0] * w.real - a[1] * w.imag, a[0] * w.imag + a[1] * w.real)


def dft2(a, b):
    return add(a, b), sub(a, b)


def dft3(a, b, c):
    s = add(b, c)
    d = sub(b, c)
    h = math.sqrt(0.75)
    m = (a[0] - 0.5 * s[0], a[1] - 0.5 * s[1])
    e = (h * d[1], -h * d[0])
    return add(a, s), add(m, e), sub(m, e)


def dft4(a, b, c, d):
    p, q = dft2(a, c)
    r, s = dft2(b, d)
    s = minus_i(s)
    return add(p, r), add(q, s), sub(p, r), sub(q, s)


def dft6(z):
    even = dft3(z[0], z[2], z[4])
    odd = dft3(z[3], z[5], z[1])
    out = [None] * 6
    for k in range(6):
        f = add if k % 2 == 0 else sub
        out[k] = f(even[k % 3], odd[k % 3])
    return out


def dft16(z):
    cols = [dft4(z[i], z[i + 4], z[i + 8], z[i + 12]) for i in range(4)]
    out = [None] * 16
    for k1 in range(4):
        row = []
        for i in range(4):
            e = (i * k1) % 16
            row.append(cols[i][k1] if e == 0 else by_const(cols[i][k1], np.exp(-2j * np.pi * e / 16)))
        res = dft4(*row)
        for k2 in range(4):
            out[k1 + 4 * k2] = res[k2]
    return out


def enter_kernel(me_ref, re_ref, im_ref, kerr_ref, out_ref, phase_ref):
    top = (me_ref[0] // 8) * 384 + pl.program_id(0) * 128
    left = (me_ref[0] % 8) * 768
    ax = chirp_angle(top + lax.broadcasted_iota(jnp.int32, (128, 128), 0))
    for lb in range(6):
        ay = chirp_angle(left + 128 * lb + lax.broadcasted_iota(jnp.int32, (1, 128), 1))
        cols = slice(128 * lb, 128 * lb + 128)
        re, im = re_ref[:, cols], im_ref[:, cols]
        phase = kerr_ref[:, cols] * (re * re + im * im)
        phase_ref[:, cols] = phase
        s, c = sin_cos(phase + (ax + ay))
        both = turn((re, im), (c, s))
        for p in range(2):
            turned = both[p].T
            for i in range(8):
                l = 128 * lb + 16 * i
                out_ref[l // 48, pl.ds(48 * p + l % 48, 16), :] = turned[16 * i:16 * i + 16]


def columns_kernel(in_ref, tw_ref, l_ref, out_ref, z_ref, high_ref, low_ref):

    def body(lh, _):
        low = pl.ds(pl.multiple_of(8 * lh, 8), 8)
        high = pl.ds(pl.multiple_of(48 + 8 * lh, 8), 8)
        for j3 in range(3):
            lanes = slice(128 * j3, 128 * j3 + 128)
            at = [(n + 5 * j3) % 16 for n in range(16)]
            z = dft16([(in_ref[r, low, lanes], in_ref[r, high, lanes]) for r in at])
            for k in range(16):
                z_ref[j3, k, 0] = z[k][0]
                z_ref[j3, k, 1] = z[k][1]
        for k in range(0, 16, 2):
            found = {}
            for m in (k, k + 1):
                z = dft3(*[(z_ref[j3, m, 0], z_ref[j3, m, 1]) for j3 in range(3)])
                for k3 in range(3):
                    rho = next(r for r in range(48) if r % 16 == m and r % 3 == k3)
                    found[rho] = turn(z[k3], (tw_ref[0, rho], tw_ref[1, rho]))
            for rho in sorted(found):
                if rho % 2 == 0:
                    rows = slice(8 * rho, 8 * rho + 16)
                    for p in range(2):
                        h, l = split(jnp.concatenate([found[rho][p], found[rho + 1][p]], 0))
                        high_ref[rows, 128 * p:128 * p + 128] = h
                        low_ref[rows, 128 * p:128 * p + 128] = l
        res = dot_left((l_ref[0], l_ref[1]), (high_ref[...], low_ref[...]), NT)
        for j in range(3):
            for p in range(2):
                out_ref[pl.ds(12 * j + 6 * p + lh, 128, stride=PITCH), :] = res[128 * p:128 * p + 128, 128 * j:128 * j + 128]
        return 0

    lax.fori_loop(0, 6, body, 0)


def gather_rows(in_ref, row, pitch, count=128, first=0):
    return in_ref[pl.ds(first * pitch + row, count, stride=pitch), :]


def over_senders(in_ref, rows, pitch, table, out_ref):
    data = jnp.concatenate([jnp.concatenate([gather_rows(in_ref, r, pitch) for r in pair], 0) for pair in rows], 1)
    out_ref[:, :data.shape[1]] = dot_left(table, split(data), NN)


def after_senders(tw_ref, v_ref, y_ref, high_ref, low_ref):
    for u in range(0, 128, 16):
        z = []
        for t in range(6):
            lanes = slice(128 * t, 128 * t + 128)
            w = (tw_ref[0, t, u:u + 16, :], tw_ref[1, t, u:u + 16, :])
            z.append(turn((y_ref[u:u + 16, lanes], y_ref[128 + u:144 + u, lanes]), w))
        z = dft6(z)
        z = [z[0]] + [turn(z[t], (v_ref[0, t], v_ref[1, t])) for t in range(1, 6)]
        for t in range(6):
            for p in range(2):
                h, l = split(z[t][p])
                high_ref[t, u:u + 16, 128 * p:128 * p + 128] = h
                low_ref[t, u:u + 16, 128 * p:128 * p + 128] = l


def rows_kernel(me_ref, in_ref, kerr_ref, l_ref, tw_ref, v_ref, m_ref, ay_ref, m2_ref, v2_ref, tw2_ref, l2_ref,
                out_ref, phase_ref, y_ref, w_ref, high_ref, low_ref):

    def body(j, _):
        over_senders(in_ref, [(12 * j + t, 12 * j + 6 + t) for t in range(6)], PITCH, (l_ref[0], l_ref[1]), y_ref)
        after_senders(tw_ref, v_ref, y_ref, high_ref, low_ref)
        rows = pl.ds(pl.multiple_of(16 * j, 16), 16)
        ax = chirp_angle(48 * me_ref[0] + 16 * j + lax.broadcasted_iota(jnp.int32, (128, 128), 0) % 16)
        for t in range(6):
            z = dot_left((m_ref[0], m_ref[1]), (high_ref[t], low_ref[t]), NT)
            re, im = z[:128], z[128:]
            lanes = slice(128 * t, 128 * t + 128)
            phase = kerr_ref[:, rows, lanes].reshape(128, 128) * (re * re + im * im)
            phase_ref[:, rows, lanes] = phase.reshape(8, 16, 128)
            ay = jnp.concatenate([jnp.broadcast_to(ay_ref[t, k:k + 1, :], (16, 128)) for k in range(8)], 0)
            s, c = sin_cos(phase + (ax + ay))
            both = jnp.concatenate(turn((im, -re), (c, s)), 0)
            w_ref[t] = dot_left((m2_ref[0], m2_ref[1]), split(both), NN)
        for r in range(0, 128, 16):
            z = [(w_ref[t, r:r + 16, :], w_ref[t, 128 + r:144 + r, :]) for t in range(6)]
            z = dft6([z[0]] + [turn(z[t], (v2_ref[0, t], v2_ref[1, t])) for t in range(1, 6)])
            for t in range(6):
                q = turn(z[t], (tw2_ref[0, t], tw2_ref[1, t]))
                for p in range(2):
                    h, l = split(q[p])
                    high_ref[t, r:r + 16, 128 * p:128 * p + 128] = h
                    low_ref[t, r:r + 16, 128 * p:128 * p + 128] = l
        for t in range(6):
            res = dot_left((l2_ref[0], l2_ref[1]), (high_ref[t], low_ref[t]), NT)
            for p in range(2):
                row = 2 * j + p
                if t < 5:
                    out_ref[pl.ds(6 * t + row, 128, stride=KEPT), :] = res[128 * p:128 * p + 128]
                else:
                    y_ref[128 * p:128 * p + 128, :128] = res[128 * p:128 * p + 128]
                    for slot in range(2):
                        b = 128 * p + int(MOVED[slot][0])
                        out_ref[pl.ds(EDGE * KEPT + 6 * slot + row, 40, stride=KEPT), :] = y_ref[b:b + 40, :128]
                    out_ref[pl.ds(EDGE * KEPT + 12 + row, 4, stride=KEPT), :] = y_ref[128 * p + 40:128 * p + 44, :128]
                    out_ref[pl.ds((EDGE + 4) * KEPT + 12 + row, 4, stride=KEPT), :] = y_ref[128 * p + 84:128 * p + 88, :128]
        return 0

    lax.fori_loop(0, 3, body, 0)


def far_field_kernel(in_ref, ph_ref, l_ref, tw_ref, v_ref, r_ref, out_ref, y_ref, w_ref, high_ref, low_ref):

    def body(g, _):
        over_senders(in_ref, [(6 * g + 2 * j, 6 * g + 2 * j + 1) for j in range(3)], KEPT, (l_ref[0], l_ref[1]), y_ref)
        for u in range(0, 128, 16):
            z = []
            for t in range(3):
                lanes = slice(128 * t, 128 * t + 128)
                w = (tw_ref[0, t, u:u + 16, :], tw_ref[1, t, u:u + 16, :])
                z.append(turn((y_ref[u:u + 16, lanes], y_ref[128 + u:144 + u, lanes]), w))
            z = dft3(*z)
            z = [z[0]] + [turn(z[t], (v_ref[0, t], v_ref[1, t])) for t in range(1, 3)]
            for t in range(3):
                for p in range(2):
                    h, l = split(z[t][p])
                    high_ref[t, u:u + 16, 128 * p:128 * p + 128] = h
                    low_ref[t, u:u + 16, 128 * p:128 * p + 128] = l
        for t in range(3):
            z = dot_right((high_ref[t], low_ref[t]), (r_ref[0], r_ref[1]), NN)
            z = turn((z[:, :128], z[:, 128:]), (ph_ref[0, t, g], ph_ref[1, t, g]))
            w_ref[t] = dot_right(split(jnp.concatenate(z, 1)), (r_ref[0], r_ref[1]), NN)
        for u in range(0, 128, 16):
            z = [(w_ref[t, u:u + 16, :128], w_ref[t, u:u + 16, 128:]) for t in range(3)]
            z = dft3(z[0], *[turn(z[t], (v_ref[0, t], v_ref[1, t])) for t in range(1, 3)])
            for t in range(3):
                q = turn(z[t], (tw_ref[0, t, u:u + 16, :], tw_ref[1, t, u:u + 16, :]))
                for p in range(2):
                    y_ref[128 * p + u:128 * p + u + 16, 128 * t:128 * t + 128] = q[p]
        res = dot_left((l_ref[0], l_ref[1]), split(y_ref[...]), NN)
        for t in range(3):
            for p in range(2):
                out_ref[pl.ds(6 * g + 2 * t + p, 128, stride=KEPT), :] = res[128 * p:128 * p + 128, 128 * t:128 * t + 128]
        return 0

    lax.fori_loop(0, 5, body, 0)


def leave_kernel(in_ref, l_ref, lm_ref, tw_ref, v_ref, m_ref, out_ref, y_ref, high_ref, low_ref):

    def body(j, _):
        row = 2 * j
        over_senders(in_ref, [(6 * t + row, 6 * t + row + 1) for t in range(5)], KEPT, (l_ref[0], l_ref[1]), y_ref)
        moved = [gather_rows(in_ref, 6 * slot + row + p, KEPT, len(MOVED[slot]), EDGE) for p in range(2) for slot in range(3)]
        y_ref[:, 640:] = dot_left((lm_ref[0], lm_ref[1]), split(jnp.concatenate(moved, 0)), NN)
        after_senders(tw_ref, v_ref, y_ref, high_ref, low_ref)
        for t in range(6):
            z = dot_left((m_ref[0], m_ref[1]), (high_ref[t], low_ref[t]), NT)
            for p in range(2):
                rows = pl.ds(pl.multiple_of(48 * p + 16 * j, 16), 16)
                out_ref[:, rows, 128 * t:128 * t + 128] = z[128 * p:128 * p + 128].reshape(8, 16, 128)
        return 0

    lax.fori_loop(0, 3, body, 0)


def aperture_kernel(at_ref, pin_ref, m0_ref, m1_ref, m2_ref, hx_ref, hy_ref, out_ref):
    outer = at_ref[0]
    for g in range(5):
        if g < 3:
            moved = (m0_ref, m1_ref, m2_ref)[g]
            rows = jnp.where(outer > g, moved[...], pin_ref[8 * g:8 * g + 8, :]).astype(F32)
        else:
            rows = pin_ref[8 * g:8 * g + 8, :].astype(F32)
        for t in range(3):
            block = jnp.concatenate([rows[:, 128 * (t + 3 * k):128 * (t + 3 * k) + 128] for k in range(16)], 0)
            block = block.T
            h = turn((hx_ref[0, t], hx_ref[1, t]), (hy_ref[0, g:g + 1, :], hy_ref[1, g:g + 1, :]))
            for p in range(2):
                out_ref[p, t, g] = block * h[p]


def nbytes(a):
    return math.prod(a.shape) * jnp.dtype(a.dtype).itemsize


def call(kernel, outs, args, scratch=(), spec=None, limit=None):
    size = sum(nbytes(a) for a in args) + sum(nbytes(o) for o in jax.tree.leaves(outs))
    held = sum(math.prod(r.shape) * jnp.dtype(r.dtype).itemsize for r in scratch)
    if spec is None:
        spec = dict(in_specs=[pl.BlockSpec(memory_space=pltpu.SMEM if a.size == 1 else pltpu.VMEM) for a in args])
    return pl.pallas_call(
        kernel,
        out_shape=outs,
        scratch_shapes=list(scratch),
        compiler_params=pltpu.CompilerParams(vmem_limit_bytes=limit or size + held + 8 * 2**20),
        cost_estimate=pl.CostEstimate(flops=0, bytes_accessed=size, transcendentals=0),
        **spec,
    )(*args)


def shape(*dims):
    return jax.ShapeDtypeStruct(dims, F32)


def exchange(x, axis):
    return lax.all_to_all(x, axis, split_axis=0, concat_axis=0, tiled=True)


def move_groups(turned):
    moves = [[(int(b), EDGE + i) for i, b in enumerate(m)] for m in MOVED]
    return [lax.ppermute(turned[40:48], ("rows", "cols"), pairs) for pairs in moves]


def make_aperture(turned, moved, me, tb):
    taken = lax.dynamic_slice_in_dim(tb["taken"], me, 1)
    h_y = lax.dynamic_index_in_dim(tb["h_y"], me, 0, keepdims=False)
    return call(aperture_kernel, shape(2, 3, 5, 128, 128), (taken, turned, *moved, tb["h_x"], h_y))


def per_device(field_real, field_imag, kerr_map, pinhole):
    tb = {k: jnp.asarray(v) for k, v in TABLES.items()}
    me = lax.axis_index(("rows", "cols"))
    place = me.reshape(1)
    both = ("rows", "cols")
    strip = pl.BlockSpec((128, 768), lambda i: (i, 0))
    enter = dict(
        grid=(3,),
        in_specs=[pl.BlockSpec(memory_space=pltpu.SMEM), strip, strip, strip],
        out_specs=(pl.BlockSpec((16, 96, 128), lambda i: (0, 0, i)), strip),
    )
    sent, phase_one = call(
        enter_kernel, (shape(16, 96, 384), shape(384, 768)), (place, field_real, field_imag, kerr_map), spec=enter, limit=60 * 2**20
    )
    sent, turned = lax.optimization_barrier((sent, pinhole.T))
    cols = exchange(sent, "rows")
    moved = move_groups(turned)
    cols, kerr_part, turned, *moved = lax.optimization_barrier((cols, kerr_map.reshape(8, 48, 768), turned, *moved))
    kerr_rows = exchange(kerr_part, "cols")
    aperture = make_aperture(turned, moved, me, tb)
    sent = call(
        columns_kernel, shape(DEV * PITCH, 128), (cols, tb["tw_rho_j"], tb["l_plain"]),
        (pltpu.VMEM((3, 16, 2, 8, 128), F32), pltpu.VMEM((384, 256), BF16), pltpu.VMEM((384, 256), BF16)),
    )
    sent, kerr_rows, aperture = lax.optimization_barrier((sent, kerr_rows, aperture))
    rows = exchange(sent.reshape(DEV, PITCH, 128), both).reshape(DEV * PITCH, 128)
    pair6 = (pltpu.VMEM((6, 128, 256), BF16), pltpu.VMEM((6, 128, 256), BF16))
    sent, phase_two = call(
        rows_kernel, (shape(DEV * KEPT, 128), shape(8, 48, 768)),
        (place, rows, kerr_rows, tb["l_mixed"], tb["tw_u_a"], tb["v_6"], tb["m_first"], tb["chirp_y"], tb["m_second"], tb["v_6_rows"], tb["tw_a_u"],
         tb["l_plain"]),
        (pltpu.VMEM((256, 768), F32), pltpu.VMEM((6, 256, 128), F32)) + pair6,
    )
    far = exchange(sent.reshape(DEV, KEPT, 128), both).reshape(DEV * KEPT, 128)
    far, phase_two = lax.optimization_barrier((far, phase_two))
    phase_back = exchange(phase_two, "cols").reshape(384, 768)
    pair3 = (pltpu.VMEM((3, 128, 256), BF16), pltpu.VMEM((3, 128, 256), BF16))
    sent = call(
        far_field_kernel, shape(DEV * KEPT, 128),
        (far, aperture, tb["l_plain"], tb["tw_u_rho"], tb["v_3"], tb["r_16"]),
        (pltpu.VMEM((256, 384), F32), pltpu.VMEM((3, 128, 256), F32)) + pair3,
    )
    sent, phase_back = lax.optimization_barrier((sent, phase_back))
    near = exchange(sent.reshape(DEV, KEPT, 128), both).reshape(DEV * KEPT, 128)
    b_integral = phase_one + phase_back
    sent = call(
        leave_kernel, shape(8, 96, 768), (near, tb["l_kept"], tb["l_moved"], tb["tw_u_a"], tb["v_6"], tb["m_first"]),
        (pltpu.VMEM((256, 768), F32),) + pair6,
    )
    out = exchange(sent, "cols")
    return (out[:, :48].reshape(384, 768), out[:, 48:].reshape(384, 768), b_integral)


def solution(mesh):
    tiles = P("rows", "cols")
    return jax.shard_map(
        per_device,
        mesh=mesh,
        in_specs=(tiles, tiles, tiles, P(None, ("rows", "cols"))),
        out_specs=(tiles, tiles, tiles),
        check_vma=False,
    )
```

```python
import math

import jax
import jax.numpy as jnp
import ml_dtypes
import numpy as np
from jax import lax
from jax.experimental import pallas as pl
from jax.experimental.pallas import tpu as pltpu
from jax.sharding import PartitionSpec as P

N = 6144
DEV = 128
PITCH = 40
EDGE = 44
KEPT = 32
MOVED = (np.arange(40), np.arange(88, 128), np.array([40, 41, 42, 43, 84, 85, 86, 87]))
F32 = jnp.float32
BF16 = jnp.bfloat16
NT = (((1,), (1,)), ((), ()))
NN = (((1,), (0,)), ((), ()))


def root(period, product):
    return np.exp(-2j * np.pi * (np.asarray(product) % period) / period)


def real_form(matrix):
    return np.block([[matrix.real, -matrix.imag], [matrix.imag, matrix.real]])


def halves(matrix):
    high = matrix.astype(np.float32).astype(ml_dtypes.bfloat16)
    low = (matrix - high.astype(np.float64)).astype(ml_dtypes.bfloat16)
    return np.stack([high, low])


def planes(table):
    return np.stack([table.real, table.imag]).astype(np.float32)


def make_tables():
    t = {}
    r128 = np.arange(128)
    n1_of_src = 16 * (r128 % 8) + r128 // 8
    s128 = 1 / math.sqrt(128)
    s48 = 1 / math.sqrt(48)
    t["tw_rho_j"] = planes(root(N, np.arange(48)[:, None] * r128[None, :]).reshape(48, 1, 128) * s48)
    t["l_mixed"] = halves(real_form(root(128, r128[:, None] * n1_of_src[None, :]) * s128))
    plain = root(128, r128[:, None] * r128[None, :]) * s128
    t["l_plain"] = halves(real_form(plain))
    outer = (r128 >= EDGE) & (r128 < DEV - EDGE)
    t["l_kept"] = halves(real_form(np.where(outer[None, :], 0, plain)))
    t["l_moved"] = halves(real_form(plain[:, np.concatenate(MOVED)]))
    lane_q, lane_8 = r128 // 8, r128 % 8
    row_8, row_q = r128 // 16, r128 % 16
    same = (row_q[:, None] == lane_q[None, :]).astype(np.float64)
    eight = same * root(8, row_8[:, None] * lane_8[None, :]) * s48
    t["m_first"] = halves(real_form(eight))
    t["m_second"] = halves(real_form(eight.T))
    six = np.arange(6)
    t["v_6"] = planes(root(48, six[:, None, None] * lane_8[None, None, :]))
    t["v_6_rows"] = planes(root(48, six[:, None, None] * (np.arange(16) % 8)[None, :, None]) * np.ones((1, 1, 128)))
    a = lane_8[None, :] + 8 * six[:, None]
    t["tw_u_a"] = planes(root(N, r128[None, :, None] * a[:, None, :]))
    a = np.arange(16)[None, :] % 8 + 8 * six[:, None]
    t["tw_a_u"] = planes(root(N, r128[None, None, :] * a[:, :, None]))
    keep = (lane_8[:, None] == lane_8[None, :]).astype(np.float64)
    sixteen = keep * root(16, lane_q[:, None] * lane_q[None, :]) * s48
    t["r_16"] = halves(real_form(sixteen).T)
    t["v_3"] = planes(root(48, np.arange(3)[:, None, None] * lane_q[None, None, :]))
    rho = lane_q[None, :] + 16 * np.arange(3)[:, None]
    t["tw_u_rho"] = planes(root(N, r128[None, :, None] * rho[:, None, :]))
    kx = r128[None, :, None] + 128 * (np.arange(3)[:, None, None] + 3 * lane_q[None, None, :])
    t["h_x"] = planes(root(2 * N, kx * kx))
    y = r128[None, None, :] + 128 * (six[:, None, None] + 6 * np.arange(8)[None, :, None])
    t["chirp_y"] = (math.pi / N * ((y * y + N) % (2 * N) - N)).astype(np.float32)
    taken = np.zeros(DEV, np.int32)
    ky = 48 * np.arange(DEV)[:, None] + 8 * np.arange(6)[None, :]
    for slot, m in enumerate(MOVED):
        for place, b in enumerate(m):
            taken[EDGE + place] = slot + 1
            ky[EDGE + place, slot] = 48 * b + 40
    t["taken"] = taken
    ky = ky[:, :, None] + lane_8[None, None, :]
    t["h_y"] = planes(root(2 * N, ky * ky)).transpose(1, 0, 2, 3)
    return t


TABLES = make_tables()


def chirp_angle(index):
    square = index * index
    turns = (square.astype(F32) * (0.5 / N)).astype(jnp.int32)
    return (math.pi / N) * (square - 2 * N * turns).astype(F32)


def sin_cos(angle):
    turns = jnp.floor(angle * (2.0 / math.pi) + 0.5)
    r = angle - turns * 1.5703125
    r = r - turns * 4.837512969970703e-4
    r = r - turns * 7.549789948768648e-8
    quarter = turns.astype(jnp.int32)
    r2 = r * r
    sine = r + r * r2 * (-1.6666654611e-1 + r2 * (8.3321608736e-3 + r2 * -1.9515295891e-4))
    cosine = 1.0 - 0.5 * r2 + r2 * r2 * (4.166664568298827e-2 + r2 * (-1.388731625493765e-3 + r2 * 2.443315711809948e-5))
    odd = (quarter & 1) == 1
    s = jnp.where(odd, cosine, sine)
    c = jnp.where(odd, sine, cosine)
    s = jnp.where((quarter & 2) == 2, -s, s)
    c = jnp.where(((quarter + 1) & 2) == 2, -c, c)
    return s, c


def split(x):
    high = x.astype(BF16)
    return high, (x - high.astype(F32)).astype(BF16)


def mm(a, b, dims):
    return lax.dot_general(a, b, dims, preferred_element_type=F32)


def dot_left(table, data, dims):
    left = jnp.concatenate([table[0], table[0], table[1]], 1)
    return mm(left, jnp.concatenate([data[0], data[1], data[0]], dims[0][1][0]), dims)


def dot_right(data, table, dims):
    right = jnp.concatenate([table[0], table[0], table[1]], 0)
    return mm(jnp.concatenate([data[0], data[1], data[0]], 1), right, dims)


def turn(z, w):
    return (z[0] * w[0] - z[1] * w[1], z[0] * w[1] + z[1] * w[0])


def add(a, b):
    return (a[0] + b[0], a[1] + b[1])


def sub(a, b):
    return (a[0] - b[0], a[1] - b[1])


def minus_i(a):
    return (a[1], -a[0])


def by_const(a, w):
    return (a[0] * w.real - a[1] * w.imag, a[0] * w.imag + a[1] * w.real)


def dft2(a, b):
    return add(a, b), sub(a, b)


def dft3(a, b, c):
    s = add(b, c)
    d = sub(b, c)
    h = math.sqrt(0.75)
    m = (a[0] - 0.5 * s[0], a[1] - 0.5 * s[1])
    e = (h * d[1], -h * d[0])
    return add(a, s), add(m, e), sub(m, e)


def dft4(a, b, c, d):
    p, q = dft2(a, c)
    r, s = dft2(b, d)
    s = minus_i(s)
    return add(p, r), add(q, s), sub(p, r), sub(q, s)


def dft6(z):
    even = dft3(z[0], z[2], z[4])
    odd = dft3(z[3], z[5], z[1])
    out = [None] * 6
    for k in range(6):
        f = add if k % 2 == 0 else sub
        out[k] = f(even[k % 3], odd[k % 3])
    return out


def dft16(z):
    cols = [dft4(z[i], z[i + 4], z[i + 8], z[i + 12]) for i in range(4)]
    out = [None] * 16
    for k1 in range(4):
        row = []
        for i in range(4):
            e = (i * k1) % 16
            row.append(cols[i][k1] if e == 0 else by_const(cols[i][k1], np.exp(-2j * np.pi * e / 16)))
        res = dft4(*row)
        for k2 in range(4):
            out[k1 + 4 * k2] = res[k2]
    return out


def enter_kernel(me_ref, re_ref, im_ref, kerr_ref, out_ref, phase_ref):
    top = (me_ref[0] // 8) * 384 + pl.program_id(0) * 128
    left = (me_ref[0] % 8) * 768
    ax = chirp_angle(top + lax.broadcasted_iota(jnp.int32, (128, 128), 0))
    for lb in range(6):
        ay = chirp_angle(left + 128 * lb + lax.broadcasted_iota(jnp.int32, (1, 128), 1))
        cols = slice(128 * lb, 128 * lb + 128)
        re, im = re_ref[:, cols], im_ref[:, cols]
        phase = kerr_ref[:, cols] * (re * re + im * im)
        phase_ref[:, cols] = phase
        s, c = sin_cos(phase + (ax + ay))
        both = turn((re, im), (c, s))
        for p in range(2):
            turned = both[p].T
            for i in range(8):
                l = 128 * lb + 16 * i
                out_ref[l // 48, pl.ds(48 * p + l % 48, 16), :] = turned[16 * i:16 * i + 16]


def columns_kernel(in_ref, tw_ref, l_ref, out_ref, z_ref, high_ref, low_ref):

    def body(lh, _):
        low = pl.ds(pl.multiple_of(8 * lh, 8), 8)
        high = pl.ds(pl.multiple_of(48 + 8 * lh, 8), 8)
        for j3 in range(3):
            lanes = slice(128 * j3, 128 * j3 + 128)
            at = [(n + 5 * j3) % 16 for n in range(16)]
            z = dft16([(in_ref[r, low, lanes], in_ref[r, high, lanes]) for r in at])
            for k in range(16):
                z_ref[j3, k, 0] = z[k][0]
                z_ref[j3, k, 1] = z[k][1]
        for k in range(0, 16, 2):
            found = {}
            for m in (k, k + 1):
                z = dft3(*[(z_ref[j3, m, 0], z_ref[j3, m, 1]) for j3 in range(3)])
                for k3 in range(3):
                    rho = next(r for r in range(48) if r % 16 == m and r % 3 == k3)
                    found[rho] = turn(z[k3], (tw_ref[0, rho], tw_ref[1, rho]))
            for rho in sorted(found):
                if rho % 2 == 0:
                    rows = slice(8 * rho, 8 * rho + 16)
                    for p in range(2):
                        h, l = split(jnp.concatenate([found[rho][p], found[rho + 1][p]], 0))
                        high_ref[rows, 128 * p:128 * p + 128] = h
                        low_ref[rows, 128 * p:128 * p + 128] = l
        res = dot_left((l_ref[0], l_ref[1]), (high_ref[...], low_ref[...]), NT)
        for j in range(3):
            for p in range(2):
                out_ref[pl.ds(12 * j + 6 * p + lh, 128, stride=PITCH), :] = res[128 * p:128 * p + 128, 128 * j:128 * j + 128]
        return 0

    lax.fori_loop(0, 6, body, 0)


def gather_rows(in_ref, row, pitch, count=128, first=0):
    return in_ref[pl.ds(first * pitch + row, count, stride=pitch), :]


def over_senders(in_ref, rows, pitch, table, out_ref):
    data = jnp.concatenate([jnp.concatenate([gather_rows(in_ref, r, pitch) for r in pair], 0) for pair in rows], 1)
    out_ref[:, :data.shape[1]] = dot_left(table, split(data), NN)


def flat(high_ref, low_ref):
    return high_ref[...].reshape(768, 256), low_ref[...].reshape(768, 256)


def after_senders(tw_ref, v_ref, y_ref, high_ref, low_ref):
    for u in range(0, 128, 16):
        z = []
        for t in range(6):
            lanes = slice(128 * t, 128 * t + 128)
            w = (tw_ref[0, t, u:u + 16, :], tw_ref[1, t, u:u + 16, :])
            z.append(turn((y_ref[u:u + 16, lanes], y_ref[128 + u:144 + u, lanes]), w))
        z = dft6(z)
        z = [z[0]] + [turn(z[t], (v_ref[0, t], v_ref[1, t])) for t in range(1, 6)]
        for t in range(6):
            for p in range(2):
                h, l = split(z[t][p])
                high_ref[t, u:u + 16, 128 * p:128 * p + 128] = h
                low_ref[t, u:u + 16, 128 * p:128 * p + 128] = l


def rows_kernel(me_ref, in_ref, kerr_ref, l_ref, tw_ref, v_ref, m_ref, ay_ref, m2_ref, v2_ref, tw2_ref, l2_ref,
                out_ref, phase_ref, y_ref, w_ref, e_high_ref, e_low_ref, high_ref, low_ref):

    def body(j, _):
        over_senders(in_ref, [(12 * j + t, 12 * j + 6 + t) for t in range(6)], PITCH, (l_ref[0], l_ref[1]), y_ref)
        after_senders(tw_ref, v_ref, y_ref, high_ref, low_ref)
        rows = pl.ds(pl.multiple_of(16 * j, 16), 16)
        ax = chirp_angle(48 * me_ref[0] + 16 * j + lax.broadcasted_iota(jnp.int32, (128, 128), 0) % 16)
        y_ref[...] = dot_left((m_ref[0], m_ref[1]), flat(high_ref, low_ref), NT)
        for t in range(6):
            lanes = slice(128 * t, 128 * t + 128)
            re, im = y_ref[:128, lanes], y_ref[128:, lanes]
            phase = kerr_ref[:, rows, lanes].reshape(128, 128) * (re * re + im * im)
            phase_ref[:, rows, lanes] = phase.reshape(8, 16, 128)
            ay = jnp.concatenate([jnp.broadcast_to(ay_ref[t, k:k + 1, :], (16, 128)) for k in range(8)], 0)
            s, c = sin_cos(phase + (ax + ay))
            both = turn((im, -re), (c, s))
            for p in range(2):
                h, l = split(both[p])
                e_high_ref[128 * p:128 * p + 128, lanes] = h
                e_low_ref[128 * p:128 * p + 128, lanes] = l
        w_ref[...] = dot_left((m2_ref[0], m2_ref[1]), (e_high_ref[...], e_low_ref[...]), NN)
        for r in range(0, 128, 16):
            z = [(w_ref[r:r + 16, 128 * t:128 * t + 128], w_ref[128 + r:144 + r, 128 * t:128 * t + 128]) for t in range(6)]
            z = dft6([z[0]] + [turn(z[t], (v2_ref[0, t], v2_ref[1, t])) for t in range(1, 6)])
            for t in range(6):
                q = turn(z[t], (tw2_ref[0, t], tw2_ref[1, t]))
                for p in range(2):
                    h, l = split(q[p])
                    high_ref[t, r:r + 16, 128 * p:128 * p + 128] = h
                    low_ref[t, r:r + 16, 128 * p:128 * p + 128] = l
        y_ref[...] = dot_left((l2_ref[0], l2_ref[1]), flat(high_ref, low_ref), NT)
        for t in range(6):
            for p in range(2):
                row = 2 * j + p
                if t < 5:
                    out_ref[pl.ds(6 * t + row, 128, stride=KEPT), :] = y_ref[128 * p:128 * p + 128, 128 * t:128 * t + 128]
                else:
                    for slot in range(2):
                        b = 128 * p + int(MOVED[slot][0])
                        out_ref[pl.ds(EDGE * KEPT + 6 * slot + row, 40, stride=KEPT), :] = y_ref[b:b + 40, 640:]
                    out_ref[pl.ds(EDGE * KEPT + 12 + row, 4, stride=KEPT), :] = y_ref[128 * p + 40:128 * p + 44, 640:]
                    out_ref[pl.ds((EDGE + 4) * KEPT + 12 + row, 4, stride=KEPT), :] = y_ref[128 * p + 84:128 * p + 88, 640:]
        return 0

    lax.fori_loop(0, 3, body, 0)


def far_field_kernel(in_ref, ph_ref, l_ref, tw_ref, v_ref, r_ref, out_ref, y_ref, w_ref, high_ref, low_ref):

    def body(g, _):
        over_senders(in_ref, [(6 * g + 2 * j, 6 * g + 2 * j + 1) for j in range(3)], KEPT, (l_ref[0], l_ref[1]), y_ref)
        for u in range(0, 128, 16):
            z = []
            for t in range(3):
                lanes = slice(128 * t, 128 * t + 128)
                w = (tw_ref[0, t, u:u + 16, :], tw_ref[1, t, u:u + 16, :])
                z.append(turn((y_ref[u:u + 16, lanes], y_ref[128 + u:144 + u, lanes]), w))
            z = dft3(*z)
            z = [z[0]] + [turn(z[t], (v_ref[0, t], v_ref[1, t])) for t in range(1, 3)]
            for t in range(3):
                for p in range(2):
                    h, l = split(z[t][p])
                    high_ref[t, u:u + 16, 128 * p:128 * p + 128] = h
                    low_ref[t, u:u + 16, 128 * p:128 * p + 128] = l
        for t in range(3):
            z = dot_right((high_ref[t], low_ref[t]), (r_ref[0], r_ref[1]), NN)
            z = turn((z[:, :128], z[:, 128:]), (ph_ref[0, t, g], ph_ref[1, t, g]))
            w_ref[t] = dot_right(split(jnp.concatenate(z, 1)), (r_ref[0], r_ref[1]), NN)
        for u in range(0, 128, 16):
            z = [(w_ref[t, u:u + 16, :128], w_ref[t, u:u + 16, 128:]) for t in range(3)]
            z = dft3(z[0], *[turn(z[t], (v_ref[0, t], v_ref[1, t])) for t in range(1, 3)])
            for t in range(3):
                q = turn(z[t], (tw_ref[0, t, u:u + 16, :], tw_ref[1, t, u:u + 16, :]))
                for p in range(2):
                    y_ref[128 * p + u:128 * p + u + 16, 128 * t:128 * t + 128] = q[p]
        res = dot_left((l_ref[0], l_ref[1]), split(y_ref[...]), NN)
        for t in range(3):
            for p in range(2):
                out_ref[pl.ds(6 * g + 2 * t + p, 128, stride=KEPT), :] = res[128 * p:128 * p + 128, 128 * t:128 * t + 128]
        return 0

    lax.fori_loop(0, 5, body, 0)


def leave_kernel(in_ref, l_ref, lm_ref, tw_ref, v_ref, m_ref, out_ref, y_ref, high_ref, low_ref):

    def body(j, _):
        row = 2 * j
        over_senders(in_ref, [(6 * t + row, 6 * t + row + 1) for t in range(5)], KEPT, (l_ref[0], l_ref[1]), y_ref)
        moved = [gather_rows(in_ref, 6 * slot + row + p, KEPT, len(MOVED[slot]), EDGE) for p in range(2) for slot in range(3)]
        y_ref[:, 640:] = dot_left((lm_ref[0], lm_ref[1]), split(jnp.concatenate(moved, 0)), NN)
        after_senders(tw_ref, v_ref, y_ref, high_ref, low_ref)
        z = dot_left((m_ref[0], m_ref[1]), flat(high_ref, low_ref), NT)
        for p in range(2):
            rows = pl.ds(pl.multiple_of(48 * p + 16 * j, 16), 16)
            out_ref[:, rows, :] = z[128 * p:128 * p + 128].reshape(8, 16, 768)
        return 0

    lax.fori_loop(0, 3, body, 0)


def aperture_kernel(at_ref, pin_ref, m0_ref, m1_ref, m2_ref, hx_ref, hy_ref, out_ref):
    outer = at_ref[0]
    for g in range(5):
        if g < 3:
            moved = (m0_ref, m1_ref, m2_ref)[g]
            rows = jnp.where(outer > g, moved[...], pin_ref[8 * g:8 * g + 8, :]).astype(F32)
        else:
            rows = pin_ref[8 * g:8 * g + 8, :].astype(F32)
        for t in range(3):
            block = jnp.concatenate([rows[:, 128 * (t + 3 * k):128 * (t + 3 * k) + 128] for k in range(16)], 0)
            block = block.T
            h = turn((hx_ref[0, t], hx_ref[1, t]), (hy_ref[0, g:g + 1, :], hy_ref[1, g:g + 1, :]))
            for p in range(2):
                out_ref[p, t, g] = block * h[p]


def nbytes(a):
    return math.prod(a.shape) * jnp.dtype(a.dtype).itemsize


def call(kernel, outs, args, scratch=(), spec=None, limit=None):
    size = sum(nbytes(a) for a in args) + sum(nbytes(o) for o in jax.tree.leaves(outs))
    held = sum(math.prod(r.shape) * jnp.dtype(r.dtype).itemsize for r in scratch)
    if spec is None:
        spec = dict(in_specs=[pl.BlockSpec(memory_space=pltpu.SMEM if a.size == 1 else pltpu.VMEM) for a in args])
    return pl.pallas_call(
        kernel,
        out_shape=outs,
        scratch_shapes=list(scratch),
        compiler_params=pltpu.CompilerParams(vmem_limit_bytes=limit or size + held + 8 * 2**20),
        cost_estimate=pl.CostEstimate(flops=0, bytes_accessed=size, transcendentals=0),
        **spec,
    )(*args)


def shape(*dims):
    return jax.ShapeDtypeStruct(dims, F32)


def exchange(x, axis):
    return lax.all_to_all(x, axis, split_axis=0, concat_axis=0, tiled=True)


def move_groups(turned):
    moves = [[(int(b), EDGE + i) for i, b in enumerate(m)] for m in MOVED]
    return [lax.ppermute(turned[40:48], ("rows", "cols"), pairs) for pairs in moves]


def make_aperture(turned, moved, me, tb):
    taken = lax.dynamic_slice_in_dim(tb["taken"], me, 1)
    h_y = lax.dynamic_index_in_dim(tb["h_y"], me, 0, keepdims=False)
    return call(aperture_kernel, shape(2, 3, 5, 128, 128), (taken, turned, *moved, tb["h_x"], h_y))


def per_device(field_real, field_imag, kerr_map, pinhole):
    tb = {k: jnp.asarray(v) for k, v in TABLES.items()}
    me = lax.axis_index(("rows", "cols"))
    place = me.reshape(1)
    both = ("rows", "cols")
    strip = pl.BlockSpec((128, 768), lambda i: (i, 0))
    enter = dict(
        grid=(3,),
        in_specs=[pl.BlockSpec(memory_space=pltpu.SMEM), strip, strip, strip],
        out_specs=(pl.BlockSpec((16, 96, 128), lambda i: (0, 0, i)), strip),
    )
    sent, phase_one = call(
        enter_kernel, (shape(16, 96, 384), shape(384, 768)), (place, field_real, field_imag, kerr_map), spec=enter, limit=60 * 2**20
    )
    kerr_rows = exchange(kerr_map.reshape(8, 48, 768), "cols")
    turned = pinhole.T
    aperture = make_aperture(turned, move_groups(turned), me, tb)
    sent, kerr_rows, aperture = lax.optimization_barrier((sent, kerr_rows, aperture))
    cols = exchange(sent, "rows")
    sent = call(
        columns_kernel, shape(DEV * PITCH, 128), (cols, tb["tw_rho_j"], tb["l_plain"]),
        (pltpu.VMEM((3, 16, 2, 8, 128), F32), pltpu.VMEM((384, 256), BF16), pltpu.VMEM((384, 256), BF16)),
    )
    rows = exchange(sent.reshape(DEV, PITCH, 128), both).reshape(DEV * PITCH, 128)
    pair6 = (pltpu.VMEM((6, 128, 256), BF16), pltpu.VMEM((6, 128, 256), BF16))
    sent, phase_two = call(
        rows_kernel, (shape(DEV * KEPT, 128), shape(8, 48, 768)),
        (place, rows, kerr_rows, tb["l_mixed"], tb["tw_u_a"], tb["v_6"], tb["m_first"], tb["chirp_y"], tb["m_second"], tb["v_6_rows"], tb["tw_a_u"],
         tb["l_plain"]),
        (pltpu.VMEM((256, 768), F32), pltpu.VMEM((256, 768), F32), pltpu.VMEM((256, 768), BF16), pltpu.VMEM((256, 768), BF16)) + pair6,
    )
    far = exchange(sent.reshape(DEV, KEPT, 128), both).reshape(DEV * KEPT, 128)
    far, phase_two = lax.optimization_barrier((far, phase_two))
    phase_back = exchange(phase_two, "cols").reshape(384, 768)
    pair3 = (pltpu.VMEM((3, 128, 256), BF16), pltpu.VMEM((3, 128, 256), BF16))
    sent = call(
        far_field_kernel, shape(DEV * KEPT, 128),
        (far, aperture, tb["l_plain"], tb["tw_u_rho"], tb["v_3"], tb["r_16"]),
        (pltpu.VMEM((256, 384), F32), pltpu.VMEM((3, 128, 256), F32)) + pair3,
    )
    sent, phase_back = lax.optimization_barrier((sent, phase_back))
    near = exchange(sent.reshape(DEV, KEPT, 128), both).reshape(DEV * KEPT, 128)
    b_integral = phase_one + phase_back
    sent = call(
        leave_kernel, shape(8, 96, 768), (near, tb["l_kept"], tb["l_moved"], tb["tw_u_a"], tb["v_6"], tb["m_first"]),
        (pltpu.VMEM((256, 768), F32),) + pair6,
    )
    out = exchange(sent, "cols")
    return (out[:, :48].reshape(384, 768), out[:, 48:].reshape(384, 768), b_integral)


def solution(mesh):
    tiles = P("rows", "cols")
    return jax.shard_map(
        per_device,
        mesh=mesh,
        in_specs=(tiles, tiles, tiles, P(None, ("rows", "cols"))),
        out_specs=(tiles, tiles, tiles),
        check_vma=False,
    )
```

```python
import math

import jax
import jax.numpy as jnp
import ml_dtypes
import numpy as np
from jax import lax
from jax.experimental import pallas as pl
from jax.experimental.pallas import tpu as pltpu
from jax.sharding import PartitionSpec as P

N = 6144
DEV = 128
PITCH = 40
EDGE = 44
KEPT = 32
MOVED = (np.arange(40), np.arange(88, 128), np.array([40, 41, 42, 43, 84, 85, 86, 87]))
F32 = jnp.float32
BF16 = jnp.bfloat16
NT = (((1,), (1,)), ((), ()))
NN = (((1,), (0,)), ((), ()))


def root(period, product):
    return np.exp(-2j * np.pi * (np.asarray(product) % period) / period)


def real_form(matrix):
    return np.block([[matrix.real, -matrix.imag], [matrix.imag, matrix.real]])


def halves(matrix):
    high = matrix.astype(np.float32).astype(ml_dtypes.bfloat16)
    low = (matrix - high.astype(np.float64)).astype(ml_dtypes.bfloat16)
    return np.stack([high, low])


def planes(table):
    return np.stack([table.real, table.imag]).astype(np.float32)


def make_tables():
    t = {}
    r128 = np.arange(128)
    n1_of_src = 16 * (r128 % 8) + r128 // 8
    s128 = 1 / math.sqrt(128)
    s48 = 1 / math.sqrt(48)
    t["tw_rho_j"] = planes(root(N, np.arange(48)[:, None] * r128[None, :]).reshape(48, 1, 128) * s48)
    t["l_mixed"] = halves(real_form(root(128, r128[:, None] * n1_of_src[None, :]) * s128))
    plain = root(128, r128[:, None] * r128[None, :]) * s128
    t["l_plain"] = halves(real_form(plain))
    outer = (r128 >= EDGE) & (r128 < DEV - EDGE)
    t["l_kept"] = halves(real_form(np.where(outer[None, :], 0, plain)))
    t["l_moved"] = halves(real_form(plain[:, np.concatenate(MOVED)]))
    lane_q, lane_8 = r128 // 8, r128 % 8
    row_8, row_q = r128 // 16, r128 % 16
    same = (row_q[:, None] == lane_q[None, :]).astype(np.float64)
    eight = same * root(8, row_8[:, None] * lane_8[None, :]) * s48
    t["m_first"] = halves(real_form(eight))
    t["m_second"] = halves(real_form(eight.T))
    six = np.arange(6)
    t["v_6"] = planes(root(48, six[:, None, None] * lane_8[None, None, :]))
    t["v_6_rows"] = planes(root(48, six[:, None, None] * (np.arange(16) % 8)[None, :, None]) * np.ones((1, 1, 128)))
    a = lane_8[None, :] + 8 * six[:, None]
    t["tw_u_a"] = planes(root(N, r128[None, :, None] * a[:, None, :]))
    a = np.arange(16)[None, :] % 8 + 8 * six[:, None]
    t["tw_a_u"] = planes(root(N, r128[None, None, :] * a[:, :, None]))
    keep = (lane_8[:, None] == lane_8[None, :]).astype(np.float64)
    sixteen = keep * root(16, lane_q[:, None] * lane_q[None, :]) * s48
    t["r_16"] = halves(real_form(sixteen).T)
    t["v_3"] = planes(root(48, np.arange(3)[:, None, None] * lane_q[None, None, :]))
    rho = lane_q[None, :] + 16 * np.arange(3)[:, None]
    t["tw_u_rho"] = planes(root(N, r128[None, :, None] * rho[:, None, :]))
    kx = r128[None, :, None] + 128 * (np.arange(3)[:, None, None] + 3 * lane_q[None, None, :])
    t["h_x"] = planes(root(2 * N, kx * kx))
    y = r128[None, None, :] + 128 * (six[:, None, None] + 6 * np.arange(8)[None, :, None])
    t["chirp_y"] = (math.pi / N * ((y * y + N) % (2 * N) - N)).astype(np.float32)
    taken = np.zeros(DEV, np.int32)
    ky = 48 * np.arange(DEV)[:, None] + 8 * np.arange(6)[None, :]
    for slot, m in enumerate(MOVED):
        for place, b in enumerate(m):
            taken[EDGE + place] = slot + 1
            ky[EDGE + place, slot] = 48 * b + 40
    t["taken"] = taken
    ky = ky[:, :, None] + lane_8[None, None, :]
    t["h_y"] = planes(root(2 * N, ky * ky)).transpose(1, 0, 2, 3)
    return t


TABLES = make_tables()


def chirp_angle(index):
    square = index * index
    turns = (square.astype(F32) * (0.5 / N)).astype(jnp.int32)
    return (math.pi / N) * (square - 2 * N * turns).astype(F32)


def sin_cos(angle):
    turns = jnp.floor(angle * (2.0 / math.pi) + 0.5)
    r = angle - turns * 1.5703125
    r = r - turns * 4.837512969970703e-4
    r = r - turns * 7.549789948768648e-8
    quarter = turns.astype(jnp.int32)
    r2 = r * r
    sine = r + r * r2 * (-1.6666654611e-1 + r2 * (8.3321608736e-3 + r2 * -1.9515295891e-4))
    cosine = 1.0 - 0.5 * r2 + r2 * r2 * (4.166664568298827e-2 + r2 * (-1.388731625493765e-3 + r2 * 2.443315711809948e-5))
    odd = (quarter & 1) == 1
    s = jnp.where(odd, cosine, sine)
    c = jnp.where(odd, sine, cosine)
    s = jnp.where((quarter & 2) == 2, -s, s)
    c = jnp.where(((quarter + 1) & 2) == 2, -c, c)
    return s, c


def split(x):
    high = x.astype(BF16)
    return high, (x - high.astype(F32)).astype(BF16)


def mm(a, b, dims):
    return lax.dot_general(a, b, dims, preferred_element_type=F32)


def dot_left(table, data, dims):
    left = jnp.concatenate([table[0], table[0], table[1]], 1)
    return mm(left, jnp.concatenate([data[0], data[1], data[0]], dims[0][1][0]), dims)


def dot_right(data, table, dims):
    right = jnp.concatenate([table[0], table[0], table[1]], 0)
    return mm(jnp.concatenate([data[0], data[1], data[0]], 1), right, dims)


def turn(z, w):
    return (z[0] * w[0] - z[1] * w[1], z[0] * w[1] + z[1] * w[0])


def add(a, b):
    return (a[0] + b[0], a[1] + b[1])


def sub(a, b):
    return (a[0] - b[0], a[1] - b[1])


def minus_i(a):
    return (a[1], -a[0])


def by_const(a, w):
    return (a[0] * w.real - a[1] * w.imag, a[0] * w.imag + a[1] * w.real)


def dft2(a, b):
    return add(a, b), sub(a, b)


def dft3(a, b, c):
    s = add(b, c)
    d = sub(b, c)
    h = math.sqrt(0.75)
    m = (a[0] - 0.5 * s[0], a[1] - 0.5 * s[1])
    e = (h * d[1], -h * d[0])
    return add(a, s), add(m, e), sub(m, e)


def dft4(a, b, c, d):
    p, q = dft2(a, c)
    r, s = dft2(b, d)
    s = minus_i(s)
    return add(p, r), add(q, s), sub(p, r), sub(q, s)


def dft6(z):
    even = dft3(z[0], z[2], z[4])
    odd = dft3(z[3], z[5], z[1])
    out = [None] * 6
    for k in range(6):
        f = add if k % 2 == 0 else sub
        out[k] = f(even[k % 3], odd[k % 3])
    return out


def dft16(z):
    cols = [dft4(z[i], z[i + 4], z[i + 8], z[i + 12]) for i in range(4)]
    out = [None] * 16
    for k1 in range(4):
        row = []
        for i in range(4):
            e = (i * k1) % 16
            row.append(cols[i][k1] if e == 0 else by_const(cols[i][k1], np.exp(-2j * np.pi * e / 16)))
        res = dft4(*row)
        for k2 in range(4):
            out[k1 + 4 * k2] = res[k2]
    return out


def enter_kernel(me_ref, re_ref, im_ref, kerr_ref, out_ref, phase_ref):
    top = (me_ref[0] // 8) * 384 + pl.program_id(0) * 128
    left = (me_ref[0] % 8) * 768
    ax = chirp_angle(top + lax.broadcasted_iota(jnp.int32, (128, 128), 0))
    for lb in range(6):
        ay = chirp_angle(left + 128 * lb + lax.broadcasted_iota(jnp.int32, (1, 128), 1))
        cols = slice(128 * lb, 128 * lb + 128)
        re, im = re_ref[:, cols], im_ref[:, cols]
        phase = kerr_ref[:, cols] * (re * re + im * im)
        phase_ref[:, cols] = phase
        s, c = sin_cos(phase + (ax + ay))
        both = turn((re, im), (c, s))
        for p in range(2):
            turned = both[p].T
            for i in range(8):
                l = 128 * lb + 16 * i
                out_ref[l // 48, pl.ds(48 * p + l % 48, 16), :] = turned[16 * i:16 * i + 16]


def columns_kernel(in_ref, tw_ref, l_ref, out_ref, z_ref, high_ref, low_ref):

    def body(lh, _):
        low = pl.ds(pl.multiple_of(8 * lh, 8), 8)
        high = pl.ds(pl.multiple_of(48 + 8 * lh, 8), 8)
        for j3 in range(3):
            lanes = slice(128 * j3, 128 * j3 + 128)
            at = [(n + 5 * j3) % 16 for n in range(16)]
            z = dft16([(in_ref[r, low, lanes], in_ref[r, high, lanes]) for r in at])
            for k in range(16):
                z_ref[j3, k, 0] = z[k][0]
                z_ref[j3, k, 1] = z[k][1]
        for k in range(0, 16, 2):
            found = {}
            for m in (k, k + 1):
                z = dft3(*[(z_ref[j3, m, 0], z_ref[j3, m, 1]) for j3 in range(3)])
                for k3 in range(3):
                    rho = next(r for r in range(48) if r % 16 == m and r % 3 == k3)
                    found[rho] = turn(z[k3], (tw_ref[0, rho], tw_ref[1, rho]))
            for rho in sorted(found):
                if rho % 2 == 0:
                    rows = slice(8 * rho, 8 * rho + 16)
                    for p in range(2):
                        h, l = split(jnp.concatenate([found[rho][p], found[rho + 1][p]], 0))
                        high_ref[rows, 128 * p:128 * p + 128] = h
                        low_ref[rows, 128 * p:128 * p + 128] = l
        res = dot_left((l_ref[0], l_ref[1]), (high_ref[...], low_ref[...]), NT)
        for j in range(3):
            for p in range(2):
                out_ref[pl.ds(12 * j + 6 * p + lh, 128, stride=PITCH), :] = res[128 * p:128 * p + 128, 128 * j:128 * j + 128]
        return 0

    lax.fori_loop(0, 6, body, 0)


def gather_rows(in_ref, row, pitch, count=128, first=0):
    return in_ref[pl.ds(first * pitch + row, count, stride=pitch), :]


def over_senders(in_ref, rows, pitch, table, out_ref):
    data = jnp.concatenate([jnp.concatenate([gather_rows(in_ref, r, pitch) for r in pair], 0) for pair in rows], 1)
    out_ref[:, :data.shape[1]] = dot_left(table, split(data), NN)


def skewed(steps, count):
    live = []
    for at in range(count):
        live.append(steps(at))
        live = [g for g in live if next(g, None)]
    while live:
        live = [g for g in live if next(g, None)]


def flat(high_ref, low_ref):
    return high_ref[...].reshape(768, 256), low_ref[...].reshape(768, 256)


def after_senders(tw_ref, v_ref, y_ref, high_ref, low_ref):
    for u in range(0, 128, 16):
        z = []
        for t in range(6):
            lanes = slice(128 * t, 128 * t + 128)
            w = (tw_ref[0, t, u:u + 16, :], tw_ref[1, t, u:u + 16, :])
            z.append(turn((y_ref[u:u + 16, lanes], y_ref[128 + u:144 + u, lanes]), w))
        z = dft6(z)
        z = [z[0]] + [turn(z[t], (v_ref[0, t], v_ref[1, t])) for t in range(1, 6)]
        for t in range(6):
            for p in range(2):
                h, l = split(z[t][p])
                high_ref[t, u:u + 16, 128 * p:128 * p + 128] = h
                low_ref[t, u:u + 16, 128 * p:128 * p + 128] = l


def rows_kernel(me_ref, in_ref, kerr_ref, l_ref, tw_ref, v_ref, m_ref, ay_ref, m2_ref, v2_ref, tw2_ref, l2_ref,
                out_ref, phase_ref, y_all, w_all, e_high_all, e_low_all, high_all, low_all):

    def steps(j):
        y_ref, w_ref, high_ref, low_ref = y_all.at[j], w_all.at[j], high_all.at[j], low_all.at[j]
        e_high_ref, e_low_ref = e_high_all.at[j], e_low_all.at[j]
        over_senders(in_ref, [(12 * j + t, 12 * j + 6 + t) for t in range(6)], PITCH, (l_ref[0], l_ref[1]), y_ref)
        yield True
        after_senders(tw_ref, v_ref, y_ref, high_ref, low_ref)
        yield True
        rows = pl.ds(16 * j, 16)
        ax = chirp_angle(48 * me_ref[0] + 16 * j + lax.broadcasted_iota(jnp.int32, (128, 128), 0) % 16)
        y_ref[...] = dot_left((m_ref[0], m_ref[1]), flat(high_ref, low_ref), NT)
        yield True
        for t in range(6):
            lanes = slice(128 * t, 128 * t + 128)
            re, im = y_ref[:128, lanes], y_ref[128:, lanes]
            phase = kerr_ref[:, rows, lanes].reshape(128, 128) * (re * re + im * im)
            phase_ref[:, rows, lanes] = phase.reshape(8, 16, 128)
            ay = jnp.concatenate([jnp.broadcast_to(ay_ref[t, k:k + 1, :], (16, 128)) for k in range(8)], 0)
            s, c = sin_cos(phase + (ax + ay))
            both = turn((im, -re), (c, s))
            for p in range(2):
                h, l = split(both[p])
                e_high_ref[128 * p:128 * p + 128, lanes] = h
                e_low_ref[128 * p:128 * p + 128, lanes] = l
        yield True
        w_ref[...] = dot_left((m2_ref[0], m2_ref[1]), (e_high_ref[...], e_low_ref[...]), NN)
        yield True
        for r in range(0, 128, 16):
            z = [(w_ref[r:r + 16, 128 * t:128 * t + 128], w_ref[128 + r:144 + r, 128 * t:128 * t + 128]) for t in range(6)]
            z = dft6([z[0]] + [turn(z[t], (v2_ref[0, t], v2_ref[1, t])) for t in range(1, 6)])
            for t in range(6):
                q = turn(z[t], (tw2_ref[0, t], tw2_ref[1, t]))
                for p in range(2):
                    h, l = split(q[p])
                    high_ref[t, r:r + 16, 128 * p:128 * p + 128] = h
                    low_ref[t, r:r + 16, 128 * p:128 * p + 128] = l
        yield True
        y_ref[...] = dot_left((l2_ref[0], l2_ref[1]), flat(high_ref, low_ref), NT)
        yield True
        for t in range(6):
            for p in range(2):
                row = 2 * j + p
                if t < 5:
                    out_ref[pl.ds(6 * t + row, 128, stride=KEPT), :] = y_ref[128 * p:128 * p + 128, 128 * t:128 * t + 128]
                else:
                    for slot in range(2):
                        b = 128 * p + int(MOVED[slot][0])
                        out_ref[pl.ds(EDGE * KEPT + 6 * slot + row, 40, stride=KEPT), :] = y_ref[b:b + 40, 640:]
                    out_ref[pl.ds(EDGE * KEPT + 12 + row, 4, stride=KEPT), :] = y_ref[128 * p + 40:128 * p + 44, 640:]
                    out_ref[pl.ds((EDGE + 4) * KEPT + 12 + row, 4, stride=KEPT), :] = y_ref[128 * p + 84:128 * p + 88, 640:]

    skewed(steps, 3)


def far_field_kernel(in_ref, ph_ref, l_ref, tw_ref, v_ref, r_ref, out_ref, y_ref, w_ref, high_ref, low_ref):

    def body(g, _):
        over_senders(in_ref, [(6 * g + 2 * j, 6 * g + 2 * j + 1) for j in range(3)], KEPT, (l_ref[0], l_ref[1]), y_ref)
        for u in range(0, 128, 16):
            z = []
            for t in range(3):
                lanes = slice(128 * t, 128 * t + 128)
                w = (tw_ref[0, t, u:u + 16, :], tw_ref[1, t, u:u + 16, :])
                z.append(turn((y_ref[u:u + 16, lanes], y_ref[128 + u:144 + u, lanes]), w))
            z = dft3(*z)
            z = [z[0]] + [turn(z[t], (v_ref[0, t], v_ref[1, t])) for t in range(1, 3)]
            for t in range(3):
                for p in range(2):
                    h, l = split(z[t][p])
                    high_ref[t, u:u + 16, 128 * p:128 * p + 128] = h
                    low_ref[t, u:u + 16, 128 * p:128 * p + 128] = l
        for t in range(3):
            z = dot_right((high_ref[t], low_ref[t]), (r_ref[0], r_ref[1]), NN)
            z = turn((z[:, :128], z[:, 128:]), (ph_ref[0, t, g], ph_ref[1, t, g]))
            w_ref[t] = dot_right(split(jnp.concatenate(z, 1)), (r_ref[0], r_ref[1]), NN)
        for u in range(0, 128, 16):
            z = [(w_ref[t, u:u + 16, :128], w_ref[t, u:u + 16, 128:]) for t in range(3)]
            z = dft3(z[0], *[turn(z[t], (v_ref[0, t], v_ref[1, t])) for t in range(1, 3)])
            for t in range(3):
                q = turn(z[t], (tw_ref[0, t, u:u + 16, :], tw_ref[1, t, u:u + 16, :]))
                for p in range(2):
                    y_ref[128 * p + u:128 * p + u + 16, 128 * t:128 * t + 128] = q[p]
        res = dot_left((l_ref[0], l_ref[1]), split(y_ref[...]), NN)
        for t in range(3):
            for p in range(2):
                out_ref[pl.ds(6 * g + 2 * t + p, 128, stride=KEPT), :] = res[128 * p:128 * p + 128, 128 * t:128 * t + 128]
        return 0

    lax.fori_loop(0, 5, body, 0)


def leave_kernel(in_ref, one_ref, two_ref, l_ref, lm_ref, tw_ref, v_ref, m_ref, out_ref, sum_ref, y_all, high_all, low_all):
    sum_ref[...] = one_ref[...] + two_ref[...]


    def steps(j):
        y_ref, high_ref, low_ref = y_all.at[j], high_all.at[j], low_all.at[j]
        row = 2 * j
        over_senders(in_ref, [(6 * t + row, 6 * t + row + 1) for t in range(5)], KEPT, (l_ref[0], l_ref[1]), y_ref)
        moved = [gather_rows(in_ref, 6 * slot + row + p, KEPT, len(MOVED[slot]), EDGE) for p in range(2) for slot in range(3)]
        y_ref[:, 640:] = dot_left((lm_ref[0], lm_ref[1]), split(jnp.concatenate(moved, 0)), NN)
        yield True
        after_senders(tw_ref, v_ref, y_ref, high_ref, low_ref)
        yield True
        z = dot_left((m_ref[0], m_ref[1]), flat(high_ref, low_ref), NT)
        for p in range(2):
            rows = pl.ds(48 * p + 16 * j, 16)
            out_ref[:, rows, :] = z[128 * p:128 * p + 128].reshape(8, 16, 768)

    skewed(steps, 3)


def aperture_kernel(at_ref, pin_ref, m0_ref, m1_ref, m2_ref, hx_ref, hy_ref, out_ref):
    outer = at_ref[0]
    for g in range(5):
        if g < 3:
            moved = (m0_ref, m1_ref, m2_ref)[g]
            rows = jnp.where(outer > g, moved[...], pin_ref[8 * g:8 * g + 8, :]).astype(F32)
        else:
            rows = pin_ref[8 * g:8 * g + 8, :].astype(F32)
        for t in range(3):
            block = jnp.concatenate([rows[:, 128 * (t + 3 * k):128 * (t + 3 * k) + 128] for k in range(16)], 0)
            block = block.T
            h = turn((hx_ref[0, t], hx_ref[1, t]), (hy_ref[0, g:g + 1, :], hy_ref[1, g:g + 1, :]))
            for p in range(2):
                out_ref[p, t, g] = block * h[p]


def nbytes(a):
    return math.prod(a.shape) * jnp.dtype(a.dtype).itemsize


def call(kernel, outs, args, scratch=(), spec=None, limit=None):
    size = sum(nbytes(a) for a in args) + sum(nbytes(o) for o in jax.tree.leaves(outs))
    held = sum(math.prod(r.shape) * jnp.dtype(r.dtype).itemsize for r in scratch)
    if spec is None:
        spec = dict(in_specs=[pl.BlockSpec(memory_space=pltpu.SMEM if a.size == 1 else pltpu.VMEM) for a in args])
    return pl.pallas_call(
        kernel,
        out_shape=outs,
        scratch_shapes=list(scratch),
        compiler_params=pltpu.CompilerParams(vmem_limit_bytes=limit or size + held + 8 * 2**20),
        cost_estimate=pl.CostEstimate(flops=0, bytes_accessed=size, transcendentals=0),
        **spec,
    )(*args)


def shape(*dims):
    return jax.ShapeDtypeStruct(dims, F32)


def exchange(x, axis):
    return lax.all_to_all(x, axis, split_axis=0, concat_axis=0, tiled=True)


def move_groups(turned):
    moves = [[(int(b), EDGE + i) for i, b in enumerate(m)] for m in MOVED]
    return [lax.ppermute(turned[40:48], ("rows", "cols"), pairs) for pairs in moves]


def make_aperture(turned, moved, me, tb):
    taken = lax.dynamic_slice_in_dim(tb["taken"], me, 1)
    h_y = lax.dynamic_index_in_dim(tb["h_y"], me, 0, keepdims=False)
    return call(aperture_kernel, shape(2, 3, 5, 128, 128), (taken, turned, *moved, tb["h_x"], h_y))


def per_device(field_real, field_imag, kerr_map, pinhole):
    tb = {k: jnp.asarray(v) for k, v in TABLES.items()}
    me = lax.axis_index(("rows", "cols"))
    place = me.reshape(1)
    both = ("rows", "cols")
    strip = pl.BlockSpec((128, 768), lambda i: (i, 0))
    enter = dict(
        grid=(3,),
        in_specs=[pl.BlockSpec(memory_space=pltpu.SMEM), strip, strip, strip],
        out_specs=(pl.BlockSpec((16, 96, 128), lambda i: (0, 0, i)), strip),
    )
    sent, phase_one = call(
        enter_kernel, (shape(16, 96, 384), shape(384, 768)), (place, field_real, field_imag, kerr_map), spec=enter, limit=60 * 2**20
    )
    kerr_rows = exchange(kerr_map.reshape(8, 48, 768), "cols")
    turned = pinhole.T
    aperture = make_aperture(turned, move_groups(turned), me, tb)
    sent, kerr_rows, aperture = lax.optimization_barrier((sent, kerr_rows, aperture))
    cols = exchange(sent, "rows")
    sent = call(
        columns_kernel, shape(DEV * PITCH, 128), (cols, tb["tw_rho_j"], tb["l_plain"]),
        (pltpu.VMEM((3, 16, 2, 8, 128), F32), pltpu.VMEM((384, 256), BF16), pltpu.VMEM((384, 256), BF16)),
    )
    rows = exchange(sent.reshape(DEV, PITCH, 128), both).reshape(DEV * PITCH, 128)
    pair6 = (pltpu.VMEM((3, 6, 128, 256), BF16), pltpu.VMEM((3, 6, 128, 256), BF16))
    sent, phase_two = call(
        rows_kernel, (shape(DEV * KEPT, 128), shape(8, 48, 768)),
        (place, rows, kerr_rows, tb["l_mixed"], tb["tw_u_a"], tb["v_6"], tb["m_first"], tb["chirp_y"], tb["m_second"], tb["v_6_rows"], tb["tw_a_u"],
         tb["l_plain"]),
        (pltpu.VMEM((3, 256, 768), F32), pltpu.VMEM((3, 256, 768), F32), pltpu.VMEM((3, 256, 768), BF16),
         pltpu.VMEM((3, 256, 768), BF16)) + pair6,
    )
    far = exchange(sent.reshape(DEV, KEPT, 128), both).reshape(DEV * KEPT, 128)
    far, phase_two = lax.optimization_barrier((far, phase_two))
    phase_back = exchange(phase_two, "cols").reshape(384, 768)
    pair3 = (pltpu.VMEM((3, 128, 256), BF16), pltpu.VMEM((3, 128, 256), BF16))
    sent = call(
        far_field_kernel, shape(DEV * KEPT, 128),
        (far, aperture, tb["l_plain"], tb["tw_u_rho"], tb["v_3"], tb["r_16"]),
        (pltpu.VMEM((256, 384), F32), pltpu.VMEM((3, 128, 256), F32)) + pair3,
    )
    sent, phase_back = lax.optimization_barrier((sent, phase_back))
    near = exchange(sent.reshape(DEV, KEPT, 128), both).reshape(DEV * KEPT, 128)
    sent, b_integral = call(
        leave_kernel, (shape(8, 96, 768), shape(384, 768)), (near, phase_one, phase_back, tb["l_kept"], tb["l_moved"], tb["tw_u_a"], tb["v_6"], tb["m_first"]),
        (pltpu.VMEM((3, 256, 768), F32),) + pair6,
    )
    out = exchange(sent, "cols")
    return (out[:, :48].reshape(384, 768), out[:, 48:].reshape(384, 768), b_integral)


def solution(mesh):
    tiles = P("rows", "cols")
    return jax.shard_map(
        per_device,
        mesh=mesh,
        in_specs=(tiles, tiles, tiles, P(None, ("rows", "cols"))),
        out_specs=(tiles, tiles, tiles),
        check_vma=False,
    )
```

```python
import math

import jax
import jax.numpy as jnp
import ml_dtypes
import numpy as np
from jax import lax
from jax.experimental import pallas as pl
from jax.experimental.pallas import tpu as pltpu
from jax.sharding import PartitionSpec as P

N = 6144
DEV = 128
PITCH = 40
EDGE = 44
KEPT = 32
MOVED = (np.arange(40), np.arange(88, 128), np.array([40, 41, 42, 43, 84, 85, 86, 87]))
F32 = jnp.float32
BF16 = jnp.bfloat16
NT = (((1,), (1,)), ((), ()))
NN = (((1,), (0,)), ((), ()))


def root(period, product):
    return np.exp(-2j * np.pi * (np.asarray(product) % period) / period)


def real_form(matrix):
    return np.block([[matrix.real, -matrix.imag], [matrix.imag, matrix.real]])


def halves(matrix):
    high = matrix.astype(np.float32).astype(ml_dtypes.bfloat16)
    low = (matrix - high.astype(np.float64)).astype(ml_dtypes.bfloat16)
    return np.stack([high, low])


def planes(table):
    return np.stack([table.real, table.imag]).astype(np.float32)


def make_tables():
    t = {}
    r128 = np.arange(128)
    n1_of_src = 16 * (r128 % 8) + r128 // 8
    s128 = 1 / math.sqrt(128)
    s48 = 1 / math.sqrt(48)
    t["tw_rho_j"] = planes(root(N, np.arange(48)[:, None] * r128[None, :]).reshape(48, 1, 128) * s48)
    t["l_mixed"] = halves(real_form(root(128, r128[:, None] * n1_of_src[None, :]) * s128))
    plain = root(128, r128[:, None] * r128[None, :]) * s128
    t["l_plain"] = halves(real_form(plain))
    outer = (r128 >= EDGE) & (r128 < DEV - EDGE)
    t["l_kept"] = halves(real_form(np.where(outer[None, :], 0, plain)))
    t["l_moved"] = halves(real_form(plain[:, np.concatenate(MOVED)]))
    lane_q, lane_8 = r128 // 8, r128 % 8
    row_8, row_q = r128 // 16, r128 % 16
    same = (row_q[:, None] == lane_q[None, :]).astype(np.float64)
    eight = same * root(8, row_8[:, None] * lane_8[None, :]) * s48
    t["m_first"] = halves(real_form(eight))
    t["m_second"] = halves(real_form(eight.T))
    six = np.arange(6)
    t["v_6"] = planes(root(48, six[:, None, None] * lane_8[None, None, :]))
    t["v_6_rows"] = planes(root(48, six[:, None, None] * (np.arange(16) % 8)[None, :, None]) * np.ones((1, 1, 128)))
    a = lane_8[None, :] + 8 * six[:, None]
    t["tw_u_a"] = planes(root(N, r128[None, :, None] * a[:, None, :]))
    a = np.arange(16)[None, :] % 8 + 8 * six[:, None]
    t["tw_a_u"] = planes(root(N, r128[None, None, :] * a[:, :, None]))
    keep = (lane_8[:, None] == lane_8[None, :]).astype(np.float64)
    sixteen = keep * root(16, lane_q[:, None] * lane_q[None, :]) * s48
    t["r_16"] = halves(real_form(sixteen).T)
    t["v_3"] = planes(root(48, np.arange(3)[:, None, None] * lane_q[None, None, :]))
    rho = lane_q[None, :] + 16 * np.arange(3)[:, None]
    t["tw_u_rho"] = planes(root(N, r128[None, :, None] * rho[:, None, :]))
    kx = r128[None, :, None] + 128 * (np.arange(3)[:, None, None] + 3 * lane_q[None, None, :])
    t["h_x"] = planes(root(2 * N, kx * kx))
    y = r128[None, None, :] + 128 * (six[:, None, None] + 6 * np.arange(8)[None, :, None])
    t["chirp_y"] = (math.pi / N * ((y * y + N) % (2 * N) - N)).astype(np.float32)
    taken = np.zeros(DEV, np.int32)
    ky = 48 * np.arange(DEV)[:, None] + 8 * np.arange(6)[None, :]
    for slot, m in enumerate(MOVED):
        for place, b in enumerate(m):
            taken[EDGE + place] = slot + 1
            ky[EDGE + place, slot] = 48 * b + 40
    t["taken"] = taken
    ky = ky[:, :, None] + lane_8[None, None, :]
    t["h_y"] = planes(root(2 * N, ky * ky)).transpose(1, 0, 2, 3)
    return t


TABLES = make_tables()


def chirp_angle(index):
    square = index * index
    turns = (square.astype(F32) * (0.5 / N)).astype(jnp.int32)
    return (math.pi / N) * (square - 2 * N * turns).astype(F32)


def sin_cos(angle):
    turns = jnp.floor(angle * (2.0 / math.pi) + 0.5)
    r = angle - turns * 1.5703125
    r = r - turns * 4.837512969970703e-4
    r = r - turns * 7.549789948768648e-8
    quarter = turns.astype(jnp.int32)
    r2 = r * r
    sine = r + r * r2 * (-1.6666654611e-1 + r2 * (8.3321608736e-3 + r2 * -1.9515295891e-4))
    cosine = 1.0 - 0.5 * r2 + r2 * r2 * (4.166664568298827e-2 + r2 * (-1.388731625493765e-3 + r2 * 2.443315711809948e-5))
    odd = (quarter & 1) == 1
    s = jnp.where(odd, cosine, sine)
    c = jnp.where(odd, sine, cosine)
    s = jnp.where((quarter & 2) == 2, -s, s)
    c = jnp.where(((quarter + 1) & 2) == 2, -c, c)
    return s, c


def split(x):
    high = x.astype(BF16)
    return high, (x - high.astype(F32)).astype(BF16)


def mm(a, b, dims):
    return lax.dot_general(a, b, dims, preferred_element_type=F32)


def dot_left(table, data, dims):
    left = jnp.concatenate([table[0], table[0], table[1]], 1)
    return mm(left, jnp.concatenate([data[0], data[1], data[0]], dims[0][1][0]), dims)


def dot_right(data, table, dims):
    right = jnp.concatenate([table[0], table[0], table[1]], 0)
    return mm(jnp.concatenate([data[0], data[1], data[0]], 1), right, dims)


def turn(z, w):
    return (z[0] * w[0] - z[1] * w[1], z[0] * w[1] + z[1] * w[0])


def add(a, b):
    return (a[0] + b[0], a[1] + b[1])


def sub(a, b):
    return (a[0] - b[0], a[1] - b[1])


def minus_i(a):
    return (a[1], -a[0])


def by_const(a, w):
    return (a[0] * w.real - a[1] * w.imag, a[0] * w.imag + a[1] * w.real)


def dft2(a, b):
    return add(a, b), sub(a, b)


def dft3(a, b, c):
    s = add(b, c)
    d = sub(b, c)
    h = math.sqrt(0.75)
    m = (a[0] - 0.5 * s[0], a[1] - 0.5 * s[1])
    e = (h * d[1], -h * d[0])
    return add(a, s), add(m, e), sub(m, e)


def dft4(a, b, c, d):
    p, q = dft2(a, c)
    r, s = dft2(b, d)
    s = minus_i(s)
    return add(p, r), add(q, s), sub(p, r), sub(q, s)


def dft6(z):
    even = dft3(z[0], z[2], z[4])
    odd = dft3(z[3], z[5], z[1])
    out = [None] * 6
    for k in range(6):
        f = add if k % 2 == 0 else sub
        out[k] = f(even[k % 3], odd[k % 3])
    return out


def dft16(z):
    cols = [dft4(z[i], z[i + 4], z[i + 8], z[i + 12]) for i in range(4)]
    out = [None] * 16
    for k1 in range(4):
        row = []
        for i in range(4):
            e = (i * k1) % 16
            row.append(cols[i][k1] if e == 0 else by_const(cols[i][k1], np.exp(-2j * np.pi * e / 16)))
        res = dft4(*row)
        for k2 in range(4):
            out[k1 + 4 * k2] = res[k2]
    return out


def enter_kernel(me_ref, re_ref, im_ref, kerr_ref, out_ref, phase_ref):
    top = (me_ref[0] // 8) * 384 + pl.program_id(0) * 128
    left = (me_ref[0] % 8) * 768
    ax = chirp_angle(top + lax.broadcasted_iota(jnp.int32, (128, 128), 0))
    for lb in range(6):
        ay = chirp_angle(left + 128 * lb + lax.broadcasted_iota(jnp.int32, (1, 128), 1))
        cols = slice(128 * lb, 128 * lb + 128)
        re, im = re_ref[:, cols], im_ref[:, cols]
        phase = kerr_ref[:, cols] * (re * re + im * im)
        phase_ref[:, cols] = phase
        s, c = sin_cos(phase + (ax + ay))
        both = turn((re, im), (c, s))
        for p in range(2):
            turned = both[p].T
            for i in range(8):
                l = 128 * lb + 16 * i
                out_ref[l // 48, pl.ds(48 * p + l % 48, 16), :] = turned[16 * i:16 * i + 16]


def columns_kernel(in_ref, tw_ref, l_ref, out_ref, z_all, high_all, low_all):
    def steps(at):
        z_ref, high_ref, low_ref = z_all.at[at], high_all.at[at], low_all.at[at]
        for half in range(2):
            low = 8 * (2 * at + half)
            for j3 in range(3):
                lanes = slice(128 * j3, 128 * j3 + 128)
                order = [(n + 5 * j3) % 16 for n in range(16)]
                z = dft16([(in_ref[r, low:low + 8, lanes], in_ref[r, 48 + low:56 + low, lanes]) for r in order])
                for k in range(16):
                    z_ref[half, j3, k, 0] = z[k][0]
                    z_ref[half, j3, k, 1] = z[k][1]
        yield True
        for half in range(2):
            for k in range(0, 16, 2):
                found = {}
                for m in (k, k + 1):
                    z = dft3(*[(z_ref[half, j3, m, 0], z_ref[half, j3, m, 1]) for j3 in range(3)])
                    for k3 in range(3):
                        rho = next(r for r in range(48) if r % 16 == m and r % 3 == k3)
                        found[rho] = turn(z[k3], (tw_ref[0, rho], tw_ref[1, rho]))
                for rho in sorted(found):
                    if rho % 2 == 0:
                        rows = slice(384 * half + 8 * rho, 384 * half + 8 * rho + 16)
                        for p in range(2):
                            h, l = split(jnp.concatenate([found[rho][p], found[rho + 1][p]], 0))
                            high_ref[rows, 128 * p:128 * p + 128] = h
                            low_ref[rows, 128 * p:128 * p + 128] = l
        yield True
        res = dot_left((l_ref[0], l_ref[1]), (high_ref[...], low_ref[...]), NT)
        for half in range(2):
            for j in range(3):
                lanes = slice(384 * half + 128 * j, 384 * half + 128 * j + 128)
                for p in range(2):
                    start = 12 * j + 6 * p + 2 * at + half
                    out_ref[pl.ds(start, 128, stride=PITCH), :] = res[128 * p:128 * p + 128, lanes]

    skewed(steps, 3)


def gather_rows(in_ref, row, pitch, count=128, first=0):
    return in_ref[pl.ds(first * pitch + row, count, stride=pitch), :]


def over_senders(in_ref, rows, pitch, table, out_ref):
    data = jnp.concatenate([jnp.concatenate([gather_rows(in_ref, r, pitch) for r in pair], 0) for pair in rows], 1)
    out_ref[:, :data.shape[1]] = dot_left(table, split(data), NN)


def skewed(steps, count):
    live = []
    for at in range(count):
        live.append(steps(at))
        live = [g for g in live if next(g, None)]
    while live:
        live = [g for g in live if next(g, None)]


def flat(high_ref, low_ref):
    return high_ref[...].reshape(768, 256), low_ref[...].reshape(768, 256)


def after_senders(tw_ref, v_ref, y_ref, high_ref, low_ref):
    for u in range(0, 128, 16):
        z = []
        for t in range(6):
            lanes = slice(128 * t, 128 * t + 128)
            w = (tw_ref[0, t, u:u + 16, :], tw_ref[1, t, u:u + 16, :])
            z.append(turn((y_ref[u:u + 16, lanes], y_ref[128 + u:144 + u, lanes]), w))
        z = dft6(z)
        z = [z[0]] + [turn(z[t], (v_ref[0, t], v_ref[1, t])) for t in range(1, 6)]
        for t in range(6):
            for p in range(2):
                h, l = split(z[t][p])
                high_ref[t, u:u + 16, 128 * p:128 * p + 128] = h
                low_ref[t, u:u + 16, 128 * p:128 * p + 128] = l


def rows_kernel(me_ref, in_ref, kerr_ref, l_ref, tw_ref, v_ref, m_ref, ay_ref, m2_ref, v2_ref, tw2_ref, l2_ref,
                out_ref, phase_ref, y_all, w_all, e_high_all, e_low_all, high_all, low_all):

    def steps(j):
        y_ref, w_ref, high_ref, low_ref = y_all.at[j], w_all.at[j], high_all.at[j], low_all.at[j]
        e_high_ref, e_low_ref = e_high_all.at[j], e_low_all.at[j]
        over_senders(in_ref, [(12 * j + t, 12 * j + 6 + t) for t in range(6)], PITCH, (l_ref[0], l_ref[1]), y_ref)
        yield True
        after_senders(tw_ref, v_ref, y_ref, high_ref, low_ref)
        yield True
        rows = pl.ds(16 * j, 16)
        ax = chirp_angle(48 * me_ref[0] + 16 * j + lax.broadcasted_iota(jnp.int32, (128, 128), 0) % 16)
        y_ref[...] = dot_left((m_ref[0], m_ref[1]), flat(high_ref, low_ref), NT)
        yield True
        for t in range(6):
            lanes = slice(128 * t, 128 * t + 128)
            re, im = y_ref[:128, lanes], y_ref[128:, lanes]
            phase = kerr_ref[:, rows, lanes].reshape(128, 128) * (re * re + im * im)
            phase_ref[:, rows, lanes] = phase.reshape(8, 16, 128)
            ay = jnp.concatenate([jnp.broadcast_to(ay_ref[t, k:k + 1, :], (16, 128)) for k in range(8)], 0)
            s, c = sin_cos(phase + (ax + ay))
            both = turn((im, -re), (c, s))
            for p in range(2):
                h, l = split(both[p])
                e_high_ref[128 * p:128 * p + 128, lanes] = h
                e_low_ref[128 * p:128 * p + 128, lanes] = l
        yield True
        w_ref[...] = dot_left((m2_ref[0], m2_ref[1]), (e_high_ref[...], e_low_ref[...]), NN)
        yield True
        for r in range(0, 128, 16):
            z = [(w_ref[r:r + 16, 128 * t:128 * t + 128], w_ref[128 + r:144 + r, 128 * t:128 * t + 128]) for t in range(6)]
            z = dft6([z[0]] + [turn(z[t], (v2_ref[0, t], v2_ref[1, t])) for t in range(1, 6)])
            for t in range(6):
                q = turn(z[t], (tw2_ref[0, t], tw2_ref[1, t]))
                for p in range(2):
                    h, l = split(q[p])
                    high_ref[t, r:r + 16, 128 * p:128 * p + 128] = h
                    low_ref[t, r:r + 16, 128 * p:128 * p + 128] = l
        yield True
        y_ref[...] = dot_left((l2_ref[0], l2_ref[1]), flat(high_ref, low_ref), NT)
        yield True
        for t in range(6):
            for p in range(2):
                row = 2 * j + p
                if t < 5:
                    out_ref[pl.ds(6 * t + row, 128, stride=KEPT), :] = y_ref[128 * p:128 * p + 128, 128 * t:128 * t + 128]
                else:
                    for slot in range(2):
                        b = 128 * p + int(MOVED[slot][0])
                        out_ref[pl.ds(EDGE * KEPT + 6 * slot + row, 40, stride=KEPT), :] = y_ref[b:b + 40, 640:]
                    out_ref[pl.ds(EDGE * KEPT + 12 + row, 4, stride=KEPT), :] = y_ref[128 * p + 40:128 * p + 44, 640:]
                    out_ref[pl.ds((EDGE + 4) * KEPT + 12 + row, 4, stride=KEPT), :] = y_ref[128 * p + 84:128 * p + 88, 640:]

    skewed(steps, 3)


def far_field_kernel(in_ref, ph_ref, l_ref, tw_ref, v_ref, r_ref, out_ref, y_ref, w_ref, high_ref, low_ref):

    def body(g, _):
        over_senders(in_ref, [(6 * g + 2 * j, 6 * g + 2 * j + 1) for j in range(3)], KEPT, (l_ref[0], l_ref[1]), y_ref)
        for u in range(0, 128, 16):
            z = []
            for t in range(3):
                lanes = slice(128 * t, 128 * t + 128)
                w = (tw_ref[0, t, u:u + 16, :], tw_ref[1, t, u:u + 16, :])
                z.append(turn((y_ref[u:u + 16, lanes], y_ref[128 + u:144 + u, lanes]), w))
            z = dft3(*z)
            z = [z[0]] + [turn(z[t], (v_ref[0, t], v_ref[1, t])) for t in range(1, 3)]
            for t in range(3):
                for p in range(2):
                    h, l = split(z[t][p])
                    high_ref[t, u:u + 16, 128 * p:128 * p + 128] = h
                    low_ref[t, u:u + 16, 128 * p:128 * p + 128] = l
        for t in range(3):
            z = dot_right((high_ref[t], low_ref[t]), (r_ref[0], r_ref[1]), NN)
            z = turn((z[:, :128], z[:, 128:]), (ph_ref[0, t, g], ph_ref[1, t, g]))
            w_ref[t] = dot_right(split(jnp.concatenate(z, 1)), (r_ref[0], r_ref[1]), NN)
        for u in range(0, 128, 16):
            z = [(w_ref[t, u:u + 16, :128], w_ref[t, u:u + 16, 128:]) for t in range(3)]
            z = dft3(z[0], *[turn(z[t], (v_ref[0, t], v_ref[1, t])) for t in range(1, 3)])
            for t in range(3):
                q = turn(z[t], (tw_ref[0, t, u:u + 16, :], tw_ref[1, t, u:u + 16, :]))
                for p in range(2):
                    y_ref[128 * p + u:128 * p + u + 16, 128 * t:128 * t + 128] = q[p]
        res = dot_left((l_ref[0], l_ref[1]), split(y_ref[...]), NN)
        for t in range(3):
            for p in range(2):
                out_ref[pl.ds(6 * g + 2 * t + p, 128, stride=KEPT), :] = res[128 * p:128 * p + 128, 128 * t:128 * t + 128]
        return 0

    lax.fori_loop(0, 5, body, 0)


def leave_kernel(in_ref, one_ref, two_ref, l_ref, lm_ref, tw_ref, v_ref, m_ref, out_ref, sum_ref, y_all, high_all, low_all):
    sum_ref[...] = one_ref[...] + two_ref[...]


    def steps(j):
        y_ref, high_ref, low_ref = y_all.at[j], high_all.at[j], low_all.at[j]
        row = 2 * j
        over_senders(in_ref, [(6 * t + row, 6 * t + row + 1) for t in range(5)], KEPT, (l_ref[0], l_ref[1]), y_ref)
        moved = [gather_rows(in_ref, 6 * slot + row + p, KEPT, len(MOVED[slot]), EDGE) for p in range(2) for slot in range(3)]
        y_ref[:, 640:] = dot_left((lm_ref[0], lm_ref[1]), split(jnp.concatenate(moved, 0)), NN)
        yield True
        after_senders(tw_ref, v_ref, y_ref, high_ref, low_ref)
        yield True
        z = dot_left((m_ref[0], m_ref[1]), flat(high_ref, low_ref), NT)
        for p in range(2):
            rows = pl.ds(48 * p + 16 * j, 16)
            out_ref[:, rows, :] = z[128 * p:128 * p + 128].reshape(8, 16, 768)

    skewed(steps, 3)


def aperture_kernel(at_ref, pin_ref, m0_ref, m1_ref, m2_ref, hx_ref, hy_ref, out_ref):
    outer = at_ref[0]
    for g in range(5):
        if g < 3:
            moved = (m0_ref, m1_ref, m2_ref)[g]
            rows = jnp.where(outer > g, moved[...], pin_ref[8 * g:8 * g + 8, :]).astype(F32)
        else:
            rows = pin_ref[8 * g:8 * g + 8, :].astype(F32)
        for t in range(3):
            block = jnp.concatenate([rows[:, 128 * (t + 3 * k):128 * (t + 3 * k) + 128] for k in range(16)], 0)
            block = block.T
            h = turn((hx_ref[0, t], hx_ref[1, t]), (hy_ref[0, g:g + 1, :], hy_ref[1, g:g + 1, :]))
            for p in range(2):
                out_ref[p, t, g] = block * h[p]


def nbytes(a):
    return math.prod(a.shape) * jnp.dtype(a.dtype).itemsize


def call(kernel, outs, args, scratch=(), spec=None, limit=None):
    size = sum(nbytes(a) for a in args) + sum(nbytes(o) for o in jax.tree.leaves(outs))
    held = sum(math.prod(r.shape) * jnp.dtype(r.dtype).itemsize for r in scratch)
    if spec is None:
        spec = dict(in_specs=[pl.BlockSpec(memory_space=pltpu.SMEM if a.size == 1 else pltpu.VMEM) for a in args])
    return pl.pallas_call(
        kernel,
        out_shape=outs,
        scratch_shapes=list(scratch),
        compiler_params=pltpu.CompilerParams(vmem_limit_bytes=limit or size + held + 8 * 2**20),
        cost_estimate=pl.CostEstimate(flops=0, bytes_accessed=size, transcendentals=0),
        **spec,
    )(*args)


def shape(*dims):
    return jax.ShapeDtypeStruct(dims, F32)


def exchange(x, axis):
    return lax.all_to_all(x, axis, split_axis=0, concat_axis=0, tiled=True)


def move_groups(turned):
    moves = [[(int(b), EDGE + i) for i, b in enumerate(m)] for m in MOVED]
    return [lax.ppermute(turned[40:48], ("rows", "cols"), pairs) for pairs in moves]


def make_aperture(turned, moved, me, tb):
    taken = lax.dynamic_slice_in_dim(tb["taken"], me, 1)
    h_y = lax.dynamic_index_in_dim(tb["h_y"], me, 0, keepdims=False)
    return call(aperture_kernel, shape(2, 3, 5, 128, 128), (taken, turned, *moved, tb["h_x"], h_y))


def per_device(field_real, field_imag, kerr_map, pinhole):
    tb = {k: jnp.asarray(v) for k, v in TABLES.items()}
    me = lax.axis_index(("rows", "cols"))
    place = me.reshape(1)
    both = ("rows", "cols")
    strip = pl.BlockSpec((128, 768), lambda i: (i, 0))
    enter = dict(
        grid=(3,),
        in_specs=[pl.BlockSpec(memory_space=pltpu.SMEM), strip, strip, strip],
        out_specs=(pl.BlockSpec((16, 96, 128), lambda i: (0, 0, i)), strip),
    )
    sent, phase_one = call(
        enter_kernel, (shape(16, 96, 384), shape(384, 768)), (place, field_real, field_imag, kerr_map), spec=enter, limit=60 * 2**20
    )
    kerr_rows = exchange(kerr_map.reshape(8, 48, 768), "cols")
    turned = pinhole.T
    aperture = make_aperture(turned, move_groups(turned), me, tb)
    sent, kerr_rows, aperture = lax.optimization_barrier((sent, kerr_rows, aperture))
    cols = exchange(sent, "rows")
    sent = call(
        columns_kernel, shape(DEV * PITCH, 128), (cols, tb["tw_rho_j"], tb["l_plain"]),
        (pltpu.VMEM((3, 2, 3, 16, 2, 8, 128), F32), pltpu.VMEM((3, 768, 256), BF16), pltpu.VMEM((3, 768, 256), BF16)),
    )
    rows = exchange(sent.reshape(DEV, PITCH, 128), both).reshape(DEV * PITCH, 128)
    pair6 = (pltpu.VMEM((3, 6, 128, 256), BF16), pltpu.VMEM((3, 6, 128, 256), BF16))
    sent, phase_two = call(
        rows_kernel, (shape(DEV * KEPT, 128), shape(8, 48, 768)),
        (place, rows, kerr_rows, tb["l_mixed"], tb["tw_u_a"], tb["v_6"], tb["m_first"], tb["chirp_y"], tb["m_second"], tb["v_6_rows"], tb["tw_a_u"],
         tb["l_plain"]),
        (pltpu.VMEM((3, 256, 768), F32), pltpu.VMEM((3, 256, 768), F32), pltpu.VMEM((3, 256, 768), BF16),
         pltpu.VMEM((3, 256, 768), BF16)) + pair6,
    )
    far = exchange(sent.reshape(DEV, KEPT, 128), both).reshape(DEV * KEPT, 128)
    far, phase_two = lax.optimization_barrier((far, phase_two))
    phase_back = exchange(phase_two, "cols").reshape(384, 768)
    pair3 = (pltpu.VMEM((3, 128, 256), BF16), pltpu.VMEM((3, 128, 256), BF16))
    sent = call(
        far_field_kernel, shape(DEV * KEPT, 128),
        (far, aperture, tb["l_plain"], tb["tw_u_rho"], tb["v_3"], tb["r_16"]),
        (pltpu.VMEM((256, 384), F32), pltpu.VMEM((3, 128, 256), F32)) + pair3,
    )
    sent, phase_back = lax.optimization_barrier((sent, phase_back))
    near = exchange(sent.reshape(DEV, KEPT, 128), both).reshape(DEV * KEPT, 128)
    sent, b_integral = call(
        leave_kernel, (shape(8, 96, 768), shape(384, 768)), (near, phase_one, phase_back, tb["l_kept"], tb["l_moved"], tb["tw_u_a"], tb["v_6"], tb["m_first"]),
        (pltpu.VMEM((3, 256, 768), F32),) + pair6,
    )
    out = exchange(sent, "cols")
    return (out[:, :48].reshape(384, 768), out[:, 48:].reshape(384, 768), b_integral)


def solution(mesh):
    tiles = P("rows", "cols")
    return jax.shard_map(
        per_device,
        mesh=mesh,
        in_specs=(tiles, tiles, tiles, P(None, ("rows", "cols"))),
        out_specs=(tiles, tiles, tiles),
        check_vma=False,
    )
```

```python
import math

import jax
import jax.numpy as jnp
import ml_dtypes
import numpy as np
from jax import lax
from jax.experimental import pallas as pl
from jax.experimental.pallas import tpu as pltpu
from jax.sharding import PartitionSpec as P

N = 6144
DEV = 128
PITCH = 40
EDGE = 44
KEPT = 32
MOVED = (np.arange(40), np.arange(88, 128), np.array([40, 41, 42, 43, 84, 85, 86, 87]))
F32 = jnp.float32
BF16 = jnp.bfloat16
NT = (((1,), (1,)), ((), ()))
NN = (((1,), (0,)), ((), ()))


def root(period, product):
    return np.exp(-2j * np.pi * (np.asarray(product) % period) / period)


def real_form(matrix):
    return np.block([[matrix.real, -matrix.imag], [matrix.imag, matrix.real]])


def halves(matrix):
    high = matrix.astype(np.float32).astype(ml_dtypes.bfloat16)
    low = (matrix - high.astype(np.float64)).astype(ml_dtypes.bfloat16)
    return np.stack([high, low])


def planes(table):
    return np.stack([table.real, table.imag]).astype(np.float32)


def make_tables():
    t = {}
    r128 = np.arange(128)
    n1_of_src = 16 * (r128 % 8) + r128 // 8
    s128 = 1 / math.sqrt(128)
    s48 = 1 / math.sqrt(48)
    t["tw_rho_j"] = planes(root(N, np.arange(48)[:, None] * r128[None, :]).reshape(48, 1, 128) * s48)
    t["l_mixed"] = halves(real_form(root(128, r128[:, None] * n1_of_src[None, :]) * s128))
    plain = root(128, r128[:, None] * r128[None, :]) * s128
    t["l_plain"] = halves(real_form(plain))
    outer = (r128 >= EDGE) & (r128 < DEV - EDGE)
    t["l_kept"] = halves(real_form(np.where(outer[None, :], 0, plain)))
    t["l_moved"] = halves(real_form(plain[:, np.concatenate(MOVED)]))
    lane_q, lane_8 = r128 // 8, r128 % 8
    row_8, row_q = r128 // 16, r128 % 16
    same = (row_q[:, None] == lane_q[None, :]).astype(np.float64)
    eight = same * root(8, row_8[:, None] * lane_8[None, :]) * s48
    t["m_first"] = halves(real_form(eight))
    t["m_second"] = halves(real_form(eight.T))
    six = np.arange(6)
    t["v_6"] = planes(root(48, six[:, None, None] * lane_8[None, None, :]))
    t["v_6_rows"] = planes(root(48, six[:, None, None] * (np.arange(16) % 8)[None, :, None]) * np.ones((1, 1, 128)))
    a = lane_8[None, :] + 8 * six[:, None]
    t["tw_u_a"] = planes(root(N, r128[None, :, None] * a[:, None, :]))
    a = np.arange(16)[None, :] % 8 + 8 * six[:, None]
    t["tw_a_u"] = planes(root(N, r128[None, None, :] * a[:, :, None]))
    keep = (lane_8[:, None] == lane_8[None, :]).astype(np.float64)
    sixteen = keep * root(16, lane_q[:, None] * lane_q[None, :]) * s48
    t["r_16"] = halves(real_form(sixteen).T)
    t["v_3"] = planes(root(48, np.arange(3)[:, None, None] * lane_q[None, None, :]))
    rho = lane_q[None, :] + 16 * np.arange(3)[:, None]
    t["tw_u_rho"] = planes(root(N, r128[None, :, None] * rho[:, None, :]))
    kx = r128[None, :, None] + 128 * (np.arange(3)[:, None, None] + 3 * lane_q[None, None, :])
    t["h_x"] = planes(root(2 * N, kx * kx))
    y = r128[None, None, :] + 128 * (six[:, None, None] + 6 * np.arange(8)[None, :, None])
    t["chirp_y"] = (2.0 / N * ((y * y + N) % (2 * N) - N)).astype(np.float32)
    taken = np.zeros(DEV, np.int32)
    ky = 48 * np.arange(DEV)[:, None] + 8 * np.arange(6)[None, :]
    for slot, m in enumerate(MOVED):
        for place, b in enumerate(m):
            taken[EDGE + place] = slot + 1
            ky[EDGE + place, slot] = 48 * b + 40
    t["taken"] = taken
    ky = ky[:, :, None] + lane_8[None, None, :]
    t["h_y"] = planes(root(2 * N, ky * ky)).transpose(1, 0, 2, 3)
    return t


TABLES = make_tables()


def chirp_angle(index):
    square = index * index
    turns = (square.astype(F32) * (0.5 / N)).astype(jnp.int32)
    return (2.0 / N) * (square - 2 * N * turns).astype(F32)


def sin_cos(angle):
    turns = jnp.floor(angle + 0.5)
    r = (angle - turns) * (math.pi / 2)
    quarter = turns.astype(jnp.int32)
    r2 = r * r
    sine = r + r * r2 * (-1.6666654611e-1 + r2 * (8.3321608736e-3 + r2 * -1.9515295891e-4))
    cosine = 1.0 - 0.5 * r2 + r2 * r2 * (4.166664568298827e-2 + r2 * (-1.388731625493765e-3 + r2 * 2.443315711809948e-5))
    odd = (quarter & 1) == 1
    s = jnp.where(odd, cosine, sine)
    c = jnp.where(odd, sine, cosine)
    s = jnp.where((quarter & 2) == 2, -s, s)
    c = jnp.where(((quarter + 1) & 2) == 2, -c, c)
    return s, c


def split(x):
    high = x.astype(BF16)
    return high, (x - high.astype(F32)).astype(BF16)


def mm(a, b, dims):
    return lax.dot_general(a, b, dims, preferred_element_type=F32)


def dot_left(table, data, dims):
    left = jnp.concatenate([table[0], table[0], table[1]], 1)
    return mm(left, jnp.concatenate([data[0], data[1], data[0]], dims[0][1][0]), dims)


def dot_right(data, table, dims):
    right = jnp.concatenate([table[0], table[0], table[1]], 0)
    return mm(jnp.concatenate([data[0], data[1], data[0]], 1), right, dims)


def turn(z, w):
    return (z[0] * w[0] - z[1] * w[1], z[0] * w[1] + z[1] * w[0])


def add(a, b):
    return (a[0] + b[0], a[1] + b[1])


def sub(a, b):
    return (a[0] - b[0], a[1] - b[1])


def minus_i(a):
    return (a[1], -a[0])


def by_const(a, w):
    return (a[0] * w.real - a[1] * w.imag, a[0] * w.imag + a[1] * w.real)


def dft2(a, b):
    return add(a, b), sub(a, b)


def dft3(a, b, c):
    s = add(b, c)
    d = sub(b, c)
    h = math.sqrt(0.75)
    m = (a[0] - 0.5 * s[0], a[1] - 0.5 * s[1])
    e = (h * d[1], -h * d[0])
    return add(a, s), add(m, e), sub(m, e)


def dft4(a, b, c, d):
    p, q = dft2(a, c)
    r, s = dft2(b, d)
    s = minus_i(s)
    return add(p, r), add(q, s), sub(p, r), sub(q, s)


def dft6(z):
    even = dft3(z[0], z[2], z[4])
    odd = dft3(z[3], z[5], z[1])
    out = [None] * 6
    for k in range(6):
        f = add if k % 2 == 0 else sub
        out[k] = f(even[k % 3], odd[k % 3])
    return out


def dft16(z):
    cols = [dft4(z[i], z[i + 4], z[i + 8], z[i + 12]) for i in range(4)]
    out = [None] * 16
    for k1 in range(4):
        row = []
        for i in range(4):
            e = (i * k1) % 16
            row.append(cols[i][k1] if e == 0 else by_const(cols[i][k1], np.exp(-2j * np.pi * e / 16)))
        res = dft4(*row)
        for k2 in range(4):
            out[k1 + 4 * k2] = res[k2]
    return out


def enter_kernel(me_ref, re_ref, im_ref, kerr_ref, out_ref, phase_ref):
    top = (me_ref[0] // 8) * 384 + pl.program_id(0) * 128
    left = (me_ref[0] % 8) * 768
    ax = chirp_angle(top + lax.broadcasted_iota(jnp.int32, (128, 128), 0))
    for lb in range(6):
        ay = chirp_angle(left + 128 * lb + lax.broadcasted_iota(jnp.int32, (1, 128), 1))
        cols = slice(128 * lb, 128 * lb + 128)
        re, im = re_ref[:, cols], im_ref[:, cols]
        phase = kerr_ref[:, cols] * (re * re + im * im)
        phase_ref[:, cols] = phase
        s, c = sin_cos(phase * (2.0 / math.pi) + (ax + ay))
        both = turn((re, im), (c, s))
        for p in range(2):
            turned = both[p].T
            for i in range(8):
                l = 128 * lb + 16 * i
                out_ref[l // 48, pl.ds(48 * p + l % 48, 16), :] = turned[16 * i:16 * i + 16]


def columns_kernel(in_ref, tw_ref, l_ref, out_ref, z_all, high_all, low_all):
    def steps(at):
        z_ref, high_ref, low_ref = z_all.at[at], high_all.at[at], low_all.at[at]
        for half in range(2):
            low = 8 * (2 * at + half)
            for j3 in range(3):
                lanes = slice(128 * j3, 128 * j3 + 128)
                order = [(n + 5 * j3) % 16 for n in range(16)]
                z = dft16([(in_ref[r, low:low + 8, lanes], in_ref[r, 48 + low:56 + low, lanes]) for r in order])
                for k in range(16):
                    z_ref[half, j3, k, 0] = z[k][0]
                    z_ref[half, j3, k, 1] = z[k][1]
        yield True
        for half in range(2):
            for k in range(0, 16, 2):
                found = {}
                for m in (k, k + 1):
                    z = dft3(*[(z_ref[half, j3, m, 0], z_ref[half, j3, m, 1]) for j3 in range(3)])
                    for k3 in range(3):
                        rho = next(r for r in range(48) if r % 16 == m and r % 3 == k3)
                        found[rho] = turn(z[k3], (tw_ref[0, rho], tw_ref[1, rho]))
                for rho in sorted(found):
                    if rho % 2 == 0:
                        rows = slice(384 * half + 8 * rho, 384 * half + 8 * rho + 16)
                        for p in range(2):
                            h, l = split(jnp.concatenate([found[rho][p], found[rho + 1][p]], 0))
                            high_ref[rows, 128 * p:128 * p + 128] = h
                            low_ref[rows, 128 * p:128 * p + 128] = l
        yield True
        res = dot_left((l_ref[0], l_ref[1]), (high_ref[...], low_ref[...]), NT)
        for half in range(2):
            for j in range(3):
                lanes = slice(384 * half + 128 * j, 384 * half + 128 * j + 128)
                for p in range(2):
                    start = 12 * j + 6 * p + 2 * at + half
                    out_ref[pl.ds(start, 128, stride=PITCH), :] = res[128 * p:128 * p + 128, lanes]

    skewed(steps, 3)


def gather_rows(in_ref, row, pitch, count=128, first=0):
    return in_ref[pl.ds(first * pitch + row, count, stride=pitch), :]


def over_senders(in_ref, rows, pitch, table, out_ref):
    data = jnp.concatenate([jnp.concatenate([gather_rows(in_ref, r, pitch) for r in pair], 0) for pair in rows], 1)
    out_ref[:, :data.shape[1]] = dot_left(table, split(data), NN)


def skewed(steps, count):
    live = []
    for at in range(count):
        live.append(steps(at))
        live = [g for g in live if next(g, None)]
    while live:
        live = [g for g in live if next(g, None)]


def flat(high_ref, low_ref):
    return high_ref[...].reshape(768, 256), low_ref[...].reshape(768, 256)


def after_senders(tw_ref, v_ref, y_ref, high_ref, low_ref):
    for u in range(0, 128, 16):
        z = []
        for t in range(6):
            lanes = slice(128 * t, 128 * t + 128)
            w = (tw_ref[0, t, u:u + 16, :], tw_ref[1, t, u:u + 16, :])
            z.append(turn((y_ref[u:u + 16, lanes], y_ref[128 + u:144 + u, lanes]), w))
        z = dft6(z)
        z = [z[0]] + [turn(z[t], (v_ref[0, t], v_ref[1, t])) for t in range(1, 6)]
        for t in range(6):
            for p in range(2):
                h, l = split(z[t][p])
                high_ref[t, u:u + 16, 128 * p:128 * p + 128] = h
                low_ref[t, u:u + 16, 128 * p:128 * p + 128] = l


def rows_kernel(me_ref, in_ref, kerr_ref, l_ref, tw_ref, v_ref, m_ref, ay_ref, m2_ref, v2_ref, tw2_ref, l2_ref,
                out_ref, phase_ref, y_all, w_all, e_high_all, e_low_all, high_all, low_all):

    def steps(j):
        y_ref, w_ref, high_ref, low_ref = y_all.at[j], w_all.at[j], high_all.at[j], low_all.at[j]
        e_high_ref, e_low_ref = e_high_all.at[j], e_low_all.at[j]
        over_senders(in_ref, [(12 * j + t, 12 * j + 6 + t) for t in range(6)], PITCH, (l_ref[0], l_ref[1]), y_ref)
        yield True
        after_senders(tw_ref, v_ref, y_ref, high_ref, low_ref)
        yield True
        rows = pl.ds(16 * j, 16)
        ax = chirp_angle(48 * me_ref[0] + 16 * j + lax.broadcasted_iota(jnp.int32, (128, 128), 0) % 16)
        y_ref[...] = dot_left((m_ref[0], m_ref[1]), flat(high_ref, low_ref), NT)
        yield True
        for t in range(6):
            lanes = slice(128 * t, 128 * t + 128)
            re, im = y_ref[:128, lanes], y_ref[128:, lanes]
            phase = kerr_ref[:, rows, lanes].reshape(128, 128) * (re * re + im * im)
            phase_ref[:, rows, lanes] = phase.reshape(8, 16, 128)
            ay = jnp.concatenate([jnp.broadcast_to(ay_ref[t, k:k + 1, :], (16, 128)) for k in range(8)], 0)
            s, c = sin_cos(phase * (2.0 / math.pi) + (ax + ay))
            both = turn((im, -re), (c, s))
            for p in range(2):
                h, l = split(both[p])
                e_high_ref[128 * p:128 * p + 128, lanes] = h
                e_low_ref[128 * p:128 * p + 128, lanes] = l
        yield True
        w_ref[...] = dot_left((m2_ref[0], m2_ref[1]), (e_high_ref[...], e_low_ref[...]), NN)
        yield True
        for r in range(0, 128, 16):
            z = [(w_ref[r:r + 16, 128 * t:128 * t + 128], w_ref[128 + r:144 + r, 128 * t:128 * t + 128]) for t in range(6)]
            z = dft6([z[0]] + [turn(z[t], (v2_ref[0, t], v2_ref[1, t])) for t in range(1, 6)])
            for t in range(6):
                q = turn(z[t], (tw2_ref[0, t], tw2_ref[1, t]))
                for p in range(2):
                    h, l = split(q[p])
                    high_ref[t, r:r + 16, 128 * p:128 * p + 128] = h
                    low_ref[t, r:r + 16, 128 * p:128 * p + 128] = l
        yield True
        y_ref[...] = dot_left((l2_ref[0], l2_ref[1]), flat(high_ref, low_ref), NT)
        yield True
        for t in range(6):
            for p in range(2):
                row = 2 * j + p
                if t < 5:
                    out_ref[pl.ds(6 * t + row, 128, stride=KEPT), :] = y_ref[128 * p:128 * p + 128, 128 * t:128 * t + 128]
                else:
                    for slot in range(2):
                        b = 128 * p + int(MOVED[slot][0])
                        out_ref[pl.ds(EDGE * KEPT + 6 * slot + row, 40, stride=KEPT), :] = y_ref[b:b + 40, 640:]
                    out_ref[pl.ds(EDGE * KEPT + 12 + row, 4, stride=KEPT), :] = y_ref[128 * p + 40:128 * p + 44, 640:]
                    out_ref[pl.ds((EDGE + 4) * KEPT + 12 + row, 4, stride=KEPT), :] = y_ref[128 * p + 84:128 * p + 88, 640:]

    skewed(steps, 3)


def far_field_kernel(in_ref, ph_ref, l_ref, tw_ref, v_ref, r_ref, out_ref, y_ref, w_ref, high_ref, low_ref):

    def body(g, _):
        over_senders(in_ref, [(6 * g + 2 * j, 6 * g + 2 * j + 1) for j in range(3)], KEPT, (l_ref[0], l_ref[1]), y_ref)
        for u in range(0, 128, 16):
            z = []
            for t in range(3):
                lanes = slice(128 * t, 128 * t + 128)
                w = (tw_ref[0, t, u:u + 16, :], tw_ref[1, t, u:u + 16, :])
                z.append(turn((y_ref[u:u + 16, lanes], y_ref[128 + u:144 + u, lanes]), w))
            z = dft3(*z)
            z = [z[0]] + [turn(z[t], (v_ref[0, t], v_ref[1, t])) for t in range(1, 3)]
            for t in range(3):
                for p in range(2):
                    h, l = split(z[t][p])
                    high_ref[t, u:u + 16, 128 * p:128 * p + 128] = h
                    low_ref[t, u:u + 16, 128 * p:128 * p + 128] = l
        for t in range(3):
            z = dot_right((high_ref[t], low_ref[t]), (r_ref[0], r_ref[1]), NN)
            z = turn((z[:, :128], z[:, 128:]), (ph_ref[0, t, g], ph_ref[1, t, g]))
            w_ref[t] = dot_right(split(jnp.concatenate(z, 1)), (r_ref[0], r_ref[1]), NN)
        for u in range(0, 128, 16):
            z = [(w_ref[t, u:u + 16, :128], w_ref[t, u:u + 16, 128:]) for t in range(3)]
            z = dft3(z[0], *[turn(z[t], (v_ref[0, t], v_ref[1, t])) for t in range(1, 3)])
            for t in range(3):
                q = turn(z[t], (tw_ref[0, t, u:u + 16, :], tw_ref[1, t, u:u + 16, :]))
                for p in range(2):
                    y_ref[128 * p + u:128 * p + u + 16, 128 * t:128 * t + 128] = q[p]
        res = dot_left((l_ref[0], l_ref[1]), split(y_ref[...]), NN)
        for t in range(3):
            for p in range(2):
                out_ref[pl.ds(6 * g + 2 * t + p, 128, stride=KEPT), :] = res[128 * p:128 * p + 128, 128 * t:128 * t + 128]
        return 0

    lax.fori_loop(0, 5, body, 0)


def leave_kernel(in_ref, one_ref, two_ref, l_ref, lm_ref, tw_ref, v_ref, m_ref, out_ref, sum_ref, y_all, high_all, low_all):
    sum_ref[...] = one_ref[...] + two_ref[...]


    def steps(j):
        y_ref, high_ref, low_ref = y_all.at[j], high_all.at[j], low_all.at[j]
        row = 2 * j
        over_senders(in_ref, [(6 * t + row, 6 * t + row + 1) for t in range(5)], KEPT, (l_ref[0], l_ref[1]), y_ref)
        moved = [gather_rows(in_ref, 6 * slot + row + p, KEPT, len(MOVED[slot]), EDGE) for p in range(2) for slot in range(3)]
        y_ref[:, 640:] = dot_left((lm_ref[0], lm_ref[1]), split(jnp.concatenate(moved, 0)), NN)
        yield True
        after_senders(tw_ref, v_ref, y_ref, high_ref, low_ref)
        yield True
        z = dot_left((m_ref[0], m_ref[1]), flat(high_ref, low_ref), NT)
        for p in range(2):
            rows = pl.ds(48 * p + 16 * j, 16)
            out_ref[:, rows, :] = z[128 * p:128 * p + 128].reshape(8, 16, 768)

    skewed(steps, 3)


def aperture_kernel(at_ref, pin_ref, m0_ref, m1_ref, m2_ref, hx_ref, hy_ref, out_ref):
    outer = at_ref[0]
    for g in range(5):
        if g < 3:
            moved = (m0_ref, m1_ref, m2_ref)[g]
            rows = jnp.where(outer > g, moved[...], pin_ref[8 * g:8 * g + 8, :]).astype(F32)
        else:
            rows = pin_ref[8 * g:8 * g + 8, :].astype(F32)
        for t in range(3):
            block = jnp.concatenate([rows[:, 128 * (t + 3 * k):128 * (t + 3 * k) + 128] for k in range(16)], 0)
            block = block.T
            h = turn((hx_ref[0, t], hx_ref[1, t]), (hy_ref[0, g:g + 1, :], hy_ref[1, g:g + 1, :]))
            for p in range(2):
                out_ref[p, t, g] = block * h[p]


def nbytes(a):
    return math.prod(a.shape) * jnp.dtype(a.dtype).itemsize


def call(kernel, outs, args, scratch=(), spec=None, limit=None):
    size = sum(nbytes(a) for a in args) + sum(nbytes(o) for o in jax.tree.leaves(outs))
    held = sum(math.prod(r.shape) * jnp.dtype(r.dtype).itemsize for r in scratch)
    if spec is None:
        spec = dict(in_specs=[pl.BlockSpec(memory_space=pltpu.SMEM if a.size == 1 else pltpu.VMEM) for a in args])
    return pl.pallas_call(
        kernel,
        out_shape=outs,
        scratch_shapes=list(scratch),
        compiler_params=pltpu.CompilerParams(vmem_limit_bytes=limit or size + held + 8 * 2**20),
        cost_estimate=pl.CostEstimate(flops=0, bytes_accessed=size, transcendentals=0),
        **spec,
    )(*args)


def shape(*dims):
    return jax.ShapeDtypeStruct(dims, F32)


def exchange(x, axis):
    return lax.all_to_all(x, axis, split_axis=0, concat_axis=0, tiled=True)


def move_groups(turned):
    moves = [[(int(b), EDGE + i) for i, b in enumerate(m)] for m in MOVED]
    return [lax.ppermute(turned[40:48], ("rows", "cols"), pairs) for pairs in moves]


def make_aperture(turned, moved, me, tb):
    taken = lax.dynamic_slice_in_dim(tb["taken"], me, 1)
    h_y = lax.dynamic_index_in_dim(tb["h_y"], me, 0, keepdims=False)
    return call(aperture_kernel, shape(2, 3, 5, 128, 128), (taken, turned, *moved, tb["h_x"], h_y))


def per_device(field_real, field_imag, kerr_map, pinhole):
    tb = {k: jnp.asarray(v) for k, v in TABLES.items()}
    me = lax.axis_index(("rows", "cols"))
    place = me.reshape(1)
    both = ("rows", "cols")
    strip = pl.BlockSpec((128, 768), lambda i: (i, 0))
    enter = dict(
        grid=(3,),
        in_specs=[pl.BlockSpec(memory_space=pltpu.SMEM), strip, strip, strip],
        out_specs=(pl.BlockSpec((16, 96, 128), lambda i: (0, 0, i)), strip),
    )
    sent, phase_one = call(
        enter_kernel, (shape(16, 96, 384), shape(384, 768)), (place, field_real, field_imag, kerr_map), spec=enter, limit=60 * 2**20
    )
    kerr_rows = exchange(kerr_map.reshape(8, 48, 768), "cols")
    turned = pinhole.T
    aperture = make_aperture(turned, move_groups(turned), me, tb)
    sent, kerr_rows, aperture = lax.optimization_barrier((sent, kerr_rows, aperture))
    cols = exchange(sent, "rows")
    sent = call(
        columns_kernel, shape(DEV * PITCH, 128), (cols, tb["tw_rho_j"], tb["l_plain"]),
        (pltpu.VMEM((3, 2, 3, 16, 2, 8, 128), F32), pltpu.VMEM((3, 768, 256), BF16), pltpu.VMEM((3, 768, 256), BF16)),
    )
    rows = exchange(sent.reshape(DEV, PITCH, 128), both).reshape(DEV * PITCH, 128)
    pair6 = (pltpu.VMEM((3, 6, 128, 256), BF16), pltpu.VMEM((3, 6, 128, 256), BF16))
    sent, phase_two = call(
        rows_kernel, (shape(DEV * KEPT, 128), shape(8, 48, 768)),
        (place, rows, kerr_rows, tb["l_mixed"], tb["tw_u_a"], tb["v_6"], tb["m_first"], tb["chirp_y"], tb["m_second"], tb["v_6_rows"], tb["tw_a_u"],
         tb["l_plain"]),
        (pltpu.VMEM((3, 256, 768), F32), pltpu.VMEM((3, 256, 768), F32), pltpu.VMEM((3, 256, 768), BF16),
         pltpu.VMEM((3, 256, 768), BF16)) + pair6,
    )
    far = exchange(sent.reshape(DEV, KEPT, 128), both).reshape(DEV * KEPT, 128)
    far, phase_two = lax.optimization_barrier((far, phase_two))
    phase_back = exchange(phase_two, "cols").reshape(384, 768)
    pair3 = (pltpu.VMEM((3, 128, 256), BF16), pltpu.VMEM((3, 128, 256), BF16))
    sent = call(
        far_field_kernel, shape(DEV * KEPT, 128),
        (far, aperture, tb["l_plain"], tb["tw_u_rho"], tb["v_3"], tb["r_16"]),
        (pltpu.VMEM((256, 384), F32), pltpu.VMEM((3, 128, 256), F32)) + pair3,
    )
    sent, phase_back = lax.optimization_barrier((sent, phase_back))
    near = exchange(sent.reshape(DEV, KEPT, 128), both).reshape(DEV * KEPT, 128)
    sent, b_integral = call(
        leave_kernel, (shape(8, 96, 768), shape(384, 768)), (near, phase_one, phase_back, tb["l_kept"], tb["l_moved"], tb["tw_u_a"], tb["v_6"], tb["m_first"]),
        (pltpu.VMEM((3, 256, 768), F32),) + pair6,
    )
    out = exchange(sent, "cols")
    return (out[:, :48].reshape(384, 768), out[:, 48:].reshape(384, 768), b_integral)


def solution(mesh):
    tiles = P("rows", "cols")
    return jax.shard_map(
        per_device,
        mesh=mesh,
        in_specs=(tiles, tiles, tiles, P(None, ("rows", "cols"))),
        out_specs=(tiles, tiles, tiles),
        check_vma=False,
    )
```
